32 devices in a mesh: aa: 4 (over x, core), ba: 8 (over z, y).
Axes of the slice: x: 2, y: 2, z: 4, core: 2. Of those that a mesh axis runs over, the one named last changes fastest.
Arguments:
- tokens: bfloat16 [32768, 2048], P(('aa', 'ba')), may hold values from -42 to 42
- grad_out: bfloat16 [32768, 1024], P(('aa', 'ba')), may hold values from -6 to 6
- master_weight: float32 [2048, 1024], P(('aa', 'ba')), may hold values from -0.003 to 0.003
- first_moment: float32 [2048, 1024], P(('aa', 'ba')), may hold values from -0.6 to 0.6
- second_moment: float32 [2048, 1024], P(('aa', 'ba')), may hold values from 0.02 to 0.2
- next_tokens: bfloat16 [32768, 2048], P(('aa', 'ba')), may hold values from -72 to 72
Outputs:
- new_first: float32 [2048, 1024], P(('aa', 'ba'))
- new_second: float32 [2048, 1024], P(('aa', 'ba'))
- next_hidden: bfloat16 [32768, 512], P(('aa', 'ba'))
The draws below stay inside these ranges and needn't reach their ends.
All inputs are finite; a program needn't handle non-finite values.
Results may differ from the reference program's by a relative error of at most 0.0064.
Values may be sent and summed in bfloat16 or wider, within the bound.
No kernel may reach another device: no remote copies, remote signals or barrier semaphores. Data moves between devices by JAX's collectives and lax.ppermute only.
A program may use at most 64 MiB of HBM per device.

```python
import math
import jax
import jax.numpy as jnp
from jax import lax

D = 2048
FF = 512
QB = 128
TOK_DEV = 1024
TOKENS = 32768
N_AA = 4
N_BA = 8


def coherent_rows(key):
    sign_key, level_key = jax.random.split(jax.random.fold_in(key, 1031))
    row_sign = jnp.where(jax.random.bernoulli(sign_key, 0.5, (TOKENS, 1)), 1.0, -1.0).astype(jnp.float32)
    row_level = jnp.exp(jax.random.uniform(level_key, (N_AA * N_BA, 1), jnp.float32, -math.log(3.0), math.log(3.0)))
    row_level = jnp.repeat(row_level, TOK_DEV, axis=0)
    strength = (1.7 / TOKENS) ** 0.25
    return row_sign * row_level * strength


def draw_tokens(key, part):
    first_key = jax.random.fold_in(jax.random.fold_in(key, 7), 0)
    second_key = jax.random.fold_in(jax.random.fold_in(key, 7), 1)
    pick_key = jax.random.fold_in(jax.random.fold_in(key, 7), 3)
    size_key = jax.random.fold_in(jax.random.fold_in(key, 7), 4)
    turn_key = jax.random.fold_in(jax.random.fold_in(key, 7), 5)
    column = jnp.arange(D, dtype=jnp.float32)
    rising = 1.0 + 2.0 * column / D
    chosen = jax.random.permutation(pick_key, D) < D // 8
    magnitude = jax.random.uniform(size_key, (D,), jnp.float32, 0.5, 1.5)
    magnitude = magnitude * jnp.where(jax.random.bernoulli(turn_key, 0.5, (D,)), 1.0, -1.0)
    spread = jnp.exp(jax.random.uniform(second_key, (D,), jnp.float32, 0.0, jnp.log(3.5)))
    sample = jnp.clip(jax.random.normal(first_key, (TOKENS, D), jnp.float32), -4.0, 4.0)
    direction = jnp.where(chosen, magnitude * rising * spread, 0.0)
    values = sample * rising * spread + coherent_rows(key) * direction[None, :]
    return jnp.clip(values, -42.0, 42.0).astype(jnp.bfloat16)


def draw_grad_out(key, part):
    noise_key, size_key, turn_key = jax.random.split(jax.random.fold_in(key, 13), 3)
    magnitude = jax.random.uniform(size_key, (2 * FF,), jnp.float32, 0.5, 1.5)
    magnitude = magnitude * jnp.where(jax.random.bernoulli(turn_key, 0.5, (2 * FF,)), 1.0, -1.0)
    coherent = coherent_rows(key) * magnitude[None, :]
    sample = jnp.clip(jax.random.normal(noise_key, (TOKENS, 2 * FF), jnp.float32), -6.0, 6.0)
    values = sample + coherent
    return jnp.clip(values, -6.0, 6.0).astype(jnp.bfloat16)


def block_levels(own_key, extent, cuts, least, high):
    gain = 1.0
    for axis_at, blocks in cuts:
        heights = jax.random.uniform(jax.random.fold_in(jax.random.fold_in(own_key, 6), axis_at), (blocks,), jnp.float32, least / len(cuts), high / len(cuts))
        gain = gain * jnp.repeat(jnp.exp(heights), extent[axis_at] // blocks).reshape((-1,) + (1,) * (len(extent) - 1 - axis_at))
    return gain


def noise(stream_key, dims, scale, bound, shards=(), kind=jnp.bfloat16):
    factor_of = block_levels(stream_key, dims, shards, -0.22, 0.18) if shards else 1.0
    entries = jax.random.normal(stream_key, dims, jnp.float32) * scale * factor_of
    return jnp.minimum(jnp.maximum(entries, -bound), bound).astype(kind)


def setup_inputs(seed: int = 0) -> dict:
    streams_of = jax.random.split(jax.random.key(seed), 7)
    tokens = draw_tokens(jax.random.fold_in(streams_of[6], 71), 0)
    grad_out = draw_grad_out(jax.random.fold_in(streams_of[6], 71), 0)
    master_weight = noise(streams_of[2], (D, 2 * FF), 0.0005, 0.003, ((0, 32),), jnp.float32)
    first_moment = noise(streams_of[3], (D, 2 * FF), 0.1, 0.6, ((0, 32),), jnp.float32)
    second_moment = jnp.clip(jnp.exp(math.log(0.2) - 2.3025851 * jax.random.uniform(streams_of[4], (D, 2 * FF), jnp.float32) ** block_levels(streams_of[4], (D, 2 * FF), ((0, 32),), -0.2, 0.2)), 0.02, 0.2)
    next_tokens = noise(streams_of[5], (TOKENS, D), 12.0, 72.0, ((0, 32),))
    return {"tokens": tokens, "grad_out": grad_out, "master_weight": master_weight, "first_moment": first_moment, "second_moment": second_moment, "next_tokens": next_tokens}


def encode(matrix):
    height, width = matrix.shape
    blocks = matrix.reshape(height, width // QB, QB)
    largest = lax.optimization_barrier(jnp.max(jnp.abs(blocks), axis=2))
    scales = ((largest + 1e-06) / 448.0).astype(jnp.bfloat16)
    codes = (blocks / scales.astype(jnp.float32)[:, :, None]).astype(jnp.bfloat16)
    return (codes, scales)

def decode(codes, scales):
    height = codes.shape[0]
    values = codes.astype(jnp.float32) * scales.astype(jnp.float32)[:, :, None]
    return values.reshape(height, codes.shape[1] * codes.shape[2])

def reference(tokens, grad_out, master_weight, first_moment, second_moment, next_tokens):
    inputs = tokens.reshape(N_AA, N_BA, TOK_DEV, D)
    cotangents = grad_out.reshape(N_AA, N_BA, TOK_DEV, 2 * FF)

    def outer_step(total, inner_index):

        def inner_step(partial_value, outer_index):
            chosen = inputs[outer_index, inner_index]
            chosen_cot = cotangents[outer_index, inner_index]
            local_grad = jnp.dot(chosen.T, chosen_cot, preferred_element_type=jnp.float32)
            codes, scales = encode(local_grad)
            return (partial_value + decode(codes, scales), None)
        partial_value, unused = lax.scan(inner_step, jnp.zeros((D, 2 * FF), jnp.float32), jnp.arange(N_AA, dtype=jnp.int32))
        codes, scales = encode(partial_value)
        return (total + decode(codes, scales), None)
    gradient, unused = lax.scan(outer_step, jnp.zeros((D, 2 * FF), jnp.float32), jnp.arange(N_BA, dtype=jnp.int32))
    gate_sq = jnp.sum(gradient[:, :FF] * gradient[:, :FF])
    up_sq = jnp.sum(gradient[:, FF:] * gradient[:, FF:])
    limit = math.sqrt(D * FF)
    gate_factor = jnp.minimum(1.0, limit / jnp.sqrt(gate_sq + 1e-06))
    up_factor = jnp.minimum(1.0, limit / jnp.sqrt(up_sq + 1e-06))
    clipped = jnp.concatenate([gradient[:, :FF] * gate_factor, gradient[:, FF:] * up_factor], axis=1)
    new_first = 0.9 * first_moment + 0.1 * clipped
    new_second = 0.95 * second_moment + 0.05 * clipped * clipped
    corr_first = 1.0 - 0.9 ** 10
    corr_second = 1.0 - 0.95 ** 10
    updated = master_weight * (1.0 - 0.003 * 0.1) - 0.003 * (new_first / corr_first) / (jnp.sqrt(new_second / corr_second) + 1e-08)
    low_weight = updated.astype(jnp.bfloat16)
    projected = jnp.dot(next_tokens, low_weight, preferred_element_type=jnp.float32)
    next_hidden = (jax.nn.silu(projected[:, :FF]) * projected[:, FF:]).astype(jnp.bfloat16)
    return (new_first, new_second, next_hidden)
```

```python
import functools
import math

import jax
import jax.numpy as jnp
from jax import lax
from jax.experimental import pallas as pl
from jax.experimental.pallas import tpu as pltpu
from jax.sharding import PartitionSpec as P

D = 2048
FF = 512
AXES = ("aa", "ba")
BF16 = jnp.bfloat16
F32 = jnp.float32
VMEM_LIMIT = 40 * 1024 * 1024


class Grid:
    def __init__(self):
        outer, inner = lax.axis_size("aa"), lax.axis_size("ba")
        self.c = 2
        self.x = outer // 2
        self.y = 1
        while self.y * self.y * 4 <= inner:
            self.y *= 2
        self.z = inner // self.y
        a, b = lax.axis_index("aa"), lax.axis_index("ba")
        self.at = {"x": a // self.c, "c": a % self.c, "z": b // self.y, "y": b % self.y}
        self.size = {"x": self.x, "c": self.c, "z": self.z, "y": self.y}

    def other(self, axis, step):
        return (self.at[axis] + step) % self.size[axis]

    def send(self, value, axis, step):
        pairs = []
        for x in range(self.x):
            for c in range(self.c):
                for z in range(self.z):
                    for y in range(self.y):
                        here = {"x": x, "c": c, "z": z, "y": y}
                        there = dict(here)
                        there[axis] = (here[axis] + step) % self.size[axis]
                        pairs.append((self.index(here), self.index(there)))
        return lax.ppermute(value, AXES, pairs)

    def index(self, at):
        return ((at["x"] * self.c + at["c"]) * self.z + at["z"]) * self.y + at["y"]


def pick(value, axis, index):
    return lax.dynamic_index_in_dim(value, index, axis, keepdims=False)


def grad_kernel(core_ref, tokens_ref, cot_ref, out_ref):
    out_ref[...] = lax.dot_general(
        tokens_ref[...], cot_ref[...], (((0,), (0,)), ((), ())), preferred_element_type=F32
    ).astype(out_ref.dtype)


def grad_rows(grid, tokens, cot, core, section, dtype):
    count, depth = tokens.shape
    width = cot.shape[1] // 2
    rows = depth // (grid.x * grid.c)
    tile = min(rows, 256)
    tiles = rows // tile
    return pl.pallas_call(
        grad_kernel,
        out_shape=jax.ShapeDtypeStruct((grid.x * rows, width), dtype),
        grid_spec=pltpu.PrefetchScalarGridSpec(
            num_scalar_prefetch=1,
            grid=(grid.x, tiles),
            in_specs=[
                pl.BlockSpec((count, tile), lambda x, t, core: (0, (x * 2 + core[0]) * tiles + t)),
                pl.BlockSpec((count, width), lambda x, t, core: (0, section)),
            ],
            out_specs=pl.BlockSpec((tile, width), lambda x, t, core: (x * tiles + t, 0)),
        ),
        compiler_params=pltpu.CompilerParams(vmem_limit_bytes=VMEM_LIMIT),
        cost_estimate=pl.CostEstimate(
            flops=2 * count * grid.x * rows * width,
            bytes_accessed=count * grid.x * rows * 2 + count * width * 2 + grid.x * rows * width * 4,
            transcendentals=0,
        ),
    )(core.reshape(1).astype(jnp.int32), tokens, cot)


def reduce_axis(grid, own, received, axis, dim):
    def part(step):
        index = grid.other(axis, step)
        total = pick(own, dim, index).astype(F32)
        for value in received:
            total = total + pick(value, dim, index).astype(F32)
        return total

    arriving = [grid.send(part(step).astype(BF16), axis, step) for step in range(1, grid.size[axis])]
    return part(0), arriving


def gather_axis(grid, value, axis):
    return [value] + [grid.send(value, axis, step) for step in range(1, grid.size[axis])]


def shards(tokens, grad_out, master_weight, first_moment, second_moment, next_tokens):
    grid = Grid()
    core = grid.at["c"]
    half = grad_out.shape[1] // 2
    rows = master_weight.shape[0]
    lead = (grid.x, grid.z, grid.y, rows, half)

    sent = [grad_rows(grid, tokens, grad_out, 1 - core, s, BF16) for s in (0, 1)]
    came = [grid.send(value, "c", 1) for value in sent]
    kept = [grad_rows(grid, tokens, grad_out, core, s, F32) for s in (0, 1)]
    kept = [value.reshape(lead) for value in kept]
    came = [[value.reshape(lead)] for value in came]
    gate, gate_in = reduce_axis(grid, kept[0], came[0], "x", 0)
    up, up_in = reduce_axis(grid, kept[1], came[1], "y", 2)
    gate, gate_in = reduce_axis(grid, gate, gate_in, "y", 1)
    up, up_in = reduce_axis(grid, up, up_in, "x", 0)

    both = jnp.concatenate([gate, up], axis=2)
    both_in = [jnp.concatenate(pair, axis=2) for pair in zip(gate_in, up_in)] if len(gate_in) == len(up_in) else None
    if both_in is None:
        gate = gate + sum(v.astype(F32) for v in gate_in)
        up = up + sum(v.astype(F32) for v in up_in)
        both, both_in = jnp.concatenate([gate, up], axis=2), []
    grad, grad_in = reduce_axis(grid, both, both_in, "z", 0)
    for value in grad_in:
        grad = grad + value.astype(F32)

    squares = grad * grad
    sums = jnp.stack([jnp.sum(squares[:, :half]), jnp.sum(squares[:, half:])])
    sums = jnp.broadcast_to(sums[:, None], (2, 128))
    for axis in ("c", "x", "y", "z"):
        size, step = grid.size[axis], 1
        while step < size:
            sums = sums + grid.send(sums, axis, step)
            step *= 2
    factors = jnp.minimum(1.0, math.sqrt(D * FF) / jnp.sqrt(sums[:, 0] + 1e-06))
    clipped = jnp.concatenate([grad[:, :half] * factors[0], grad[:, half:] * factors[1]], axis=1)
    new_first = 0.9 * first_moment + 0.1 * clipped
    new_second = 0.95 * second_moment + 0.05 * clipped * clipped
    corr_first = 1.0 - 0.9**10
    corr_second = 1.0 - 0.95**10
    updated = master_weight * (1.0 - 0.003 * 0.1) - 0.003 * (new_first / corr_first) / (
        jnp.sqrt(new_second / corr_second) + 1e-08
    )
    low_weight = updated.astype(BF16)

    pieces = gather_axis(grid, low_weight, "z")
    gate = jnp.stack([p[:, :half] for p in pieces])
    up = jnp.stack([p[:, half:] for p in pieces])
    gate = jnp.stack(gather_axis(grid, gate, "y"))
    up = jnp.stack(gather_axis(grid, up, "x"))
    gates = gather_axis(grid, gate, "x")
    ups = gather_axis(grid, up, "y")
    own = (gates, ups)
    other = tuple([grid.send(v, "c", 1) for v in vs] for vs in own)
    partial = project(grid, next_tokens, own, core, None)
    next_hidden = project(grid, next_tokens, other, 1 - core, partial)
    return new_first, new_second, next_hidden


def project_body(sizes, finish, at_ref, *refs):
    nx, ny, nz, rows = sizes
    refs = list(refs)
    tokens = [refs.pop(0) for _ in range(nx)]
    gates = [refs.pop(0) for _ in range(nx)]
    ups = [refs.pop(0) for _ in range(ny)]
    before = [refs.pop(0) for _ in range(2)] if finish else None
    outs = [refs.pop(0) for _ in range(1 if finish else 2)]
    gate_w, up_w = refs
    at_x, at_y, at_z = at_ref[1], at_ref[2], at_ref[3]
    block = nz * ny * rows

    @pl.when(pl.program_id(0) == 0)
    def _():
        for kx in range(nx):
            x = lax.rem(at_x + nx - kx, nx)
            for ky in range(ny):
                y = lax.rem(at_y + ny - ky, ny)
                for kz in range(nz):
                    z = lax.rem(at_z + nz - kz, nz)
                    start = pl.multiple_of((z * ny + y) * rows, rows)
                    gate_w[x, pl.ds(start, rows), :] = gates[kx][ky, kz].astype(gate_w.dtype)
                    up_w[x, pl.ds(start, rows), :] = ups[ky][kx, kz].astype(up_w.dtype)

    gate = before[0][...] if finish else None
    up = before[1][...] if finish else None
    for x in range(nx):
        for_gate = jnp.dot(tokens[x][...], gate_w[x].astype(BF16), preferred_element_type=F32)
        for_up = jnp.dot(tokens[x][...], up_w[x].astype(BF16), preferred_element_type=F32)
        gate = for_gate if gate is None else gate + for_gate
        up = for_up if up is None else up + for_up
    if finish:
        outs[0][...] = (gate / (1.0 + jnp.exp(-gate)) * up).astype(outs[0].dtype)
    else:
        outs[0][...] = gate
        outs[1][...] = up


def project(grid, tokens, pieces, core, before):
    gates, ups = pieces
    count, depth = tokens.shape
    rows, half = gates[0].shape[-2:]
    block = depth // (grid.x * grid.c)
    tile = min(count, 256)
    finish = before is not None
    held = BF16 if rows % 16 == 0 else F32
    at = jnp.stack([core, grid.at["x"], grid.at["y"], grid.at["z"]]).astype(jnp.int32)
    token_specs = [
        pl.BlockSpec((tile, block), lambda t, at, x=x: (t, x * 2 + at[0])) for x in range(grid.x)
    ]
    whole = pl.BlockSpec(memory_space=pltpu.VMEM)
    tiled = pl.BlockSpec((tile, half), lambda t, at: (t, 0))
    wide = jax.ShapeDtypeStruct((count, half), F32)
    low = jax.ShapeDtypeStruct((count, half), BF16)
    return pl.pallas_call(
        functools.partial(project_body, (grid.x, grid.y, grid.z, rows), finish),
        out_shape=low if finish else (wide, wide),
        grid_spec=pltpu.PrefetchScalarGridSpec(
            num_scalar_prefetch=1,
            grid=(count // tile,),
            in_specs=token_specs + [whole] * (grid.x + grid.y) + ([tiled, tiled] if finish else []),
            out_specs=tiled if finish else [tiled, tiled],
            scratch_shapes=[pltpu.VMEM((grid.x, block, half), held)] * 2,
        ),
        compiler_params=pltpu.CompilerParams(vmem_limit_bytes=VMEM_LIMIT),
        cost_estimate=pl.CostEstimate(
            flops=2 * count * depth * half, bytes_accessed=count * depth + 2 * depth * half, transcendentals=0
        ),
    )(at, *([tokens] * grid.x), *gates, *ups, *(before if finish else ()))


def solution(mesh):
    spec = P(AXES, None)
    return jax.shard_map(shards, mesh=mesh, in_specs=(spec,) * 6, out_specs=(spec,) * 3, check_vma=False)
```

```python
import functools
import math

import jax
import jax.numpy as jnp
from jax import lax
from jax.experimental import pallas as pl
from jax.experimental.pallas import tpu as pltpu
from jax.sharding import PartitionSpec as P

D = 2048
FF = 512
AXES = ("aa", "ba")
BF16 = jnp.bfloat16
F32 = jnp.float32
LARGE = 60 * 1024 * 1024
SMALL = 24 * 1024 * 1024


class Grid:
    def __init__(self):
        outer, inner = lax.axis_size("aa"), lax.axis_size("ba")
        y = 1
        while y * y * 4 <= inner:
            y *= 2
        self.size = {"x": outer // 2, "c": 2, "z": inner // y, "y": y}

    def here(self, axis, step=0):
        a, b = lax.axis_index("aa"), lax.axis_index("ba")
        inner = self.size["c"] if axis in "xc" else self.size["y"]
        index = a if axis in "xc" else b
        at = lax.div(index, inner) if axis in "xz" else lax.rem(index, inner)
        return lax.rem(at + step % self.size[axis], self.size[axis]) if step else at

    def send(self, value, **steps):
        pairs = []
        for x in range(self.size["x"]):
            for c in range(self.size["c"]):
                for z in range(self.size["z"]):
                    for y in range(self.size["y"]):
                        here = {"x": x, "c": c, "z": z, "y": y}
                        there = {k: (v + steps.get(k, 0)) % self.size[k] for k, v in here.items()}
                        pairs.append((self.index(here), self.index(there)))
        return lax.ppermute(value, AXES, pairs)

    def index(self, at):
        return ((at["x"] * self.size["c"] + at["c"]) * self.size["z"] + at["z"]) * self.size["y"] + at["y"]


def pick(value, axis, index):
    return lax.dynamic_index_in_dim(value, index, axis, keepdims=False)


def kernel_params(flops, moved, limit=LARGE):
    return dict(
        compiler_params=pltpu.CompilerParams(vmem_limit_bytes=limit),
        cost_estimate=pl.CostEstimate(flops=flops, bytes_accessed=moved, transcendentals=0),
    )


def grad_kernel(tokens_ref, cot_ref, *out_refs):
    value = lax.dot_general(
        tokens_ref[...], cot_ref[...], (((0,), (0,)), ((), ())), preferred_element_type=F32
    )
    width = out_refs[0].shape[1]
    for k, ref in enumerate(out_refs):
        ref[...] = value[:, k * width : (k + 1) * width].astype(ref.dtype)


def grad_rows(grid, tokens, cot, step, dtype):
    count, depth = tokens.shape
    width = cot.shape[1] // 2
    n = grid.size["x"]
    rows = depth // (n * 2)
    shape = jax.ShapeDtypeStruct((n * rows, width), dtype)
    spec = pl.BlockSpec((rows, width), lambda x: (x, 0))
    return pl.pallas_call(
        grad_kernel,
        out_shape=[shape, shape],
        grid=(n,),
        in_specs=[
            pl.BlockSpec((count, rows), lambda x: (0, x * 2 + grid.here("c", step))),
            pl.BlockSpec((count, 2 * width), lambda x: (0, 0)),
        ],
        out_specs=[spec, spec],
        **kernel_params(
            4 * count * n * rows * width, count * n * rows * 2 + count * width * 4 + n * rows * width * 4
        ),
    )(tokens, cot)


DIM = {"x": 0, "y": 2}


def scatter_xy(grid, kept, came, order):
    one_axis, two_axis = order
    n_one, n_two = grid.size[one_axis], grid.size[two_axis]

    def pair_sum(step):
        at = grid.here(one_axis, step)
        return pick(kept, DIM[one_axis], at) + pick(came, DIM[one_axis], at).astype(F32)

    arriving = [grid.send(pair_sum(one).astype(BF16), **{one_axis: one}) for one in range(1, n_one)]
    yield
    own = pair_sum(0)
    for value in arriving:
        own = own + value.astype(F32)
    dim = 1 if two_axis == "y" else 0
    arriving = [
        grid.send(pick(own, dim, grid.here(two_axis, two)).astype(BF16), **{two_axis: two}) for two in range(1, n_two)
    ]
    yield
    total = pick(own, dim, grid.here(two_axis))
    for value in arriving:
        total = total + value.astype(F32)
    yield total


def scatter_z(grid, totals):
    whole = jnp.concatenate(totals, axis=2)
    arriving = [
        grid.send(pick(whole, 0, grid.here("z", k)).astype(BF16), z=k) for k in range(1, grid.size["z"])
    ]
    yield
    total = pick(whole, 0, grid.here("z"))
    for value in arriving:
        total = total + value.astype(F32)
    yield total


def sum_everywhere(grid, value):
    value = value + grid.send(value, c=1)
    plane = [(kx, ky) for kx in range(grid.size["x"]) for ky in range(grid.size["y"]) if kx + ky]
    value = sum([grid.send(value, x=kx, y=ky) for kx, ky in plane], value)
    return sum([grid.send(value, z=k) for k in range(1, grid.size["z"])], value)


def moments(clipped, first, second):
    return 0.9 * first + 0.1 * clipped, 0.95 * second + 0.05 * clipped * clipped


def clip_factor(square):
    return jnp.minimum(1.0, math.sqrt(D * FF) / jnp.sqrt(square + 1e-06))


def adam(clipped, weight, first, second):
    new_first, new_second = moments(clipped, first, second)
    corr_first = 1.0 - 0.9**10
    corr_second = 1.0 - 0.95**10
    updated = weight * (1.0 - 0.003 * 0.1) - 0.003 * (new_first / corr_first) / (
        jnp.sqrt(new_second / corr_second) + 1e-08
    )
    return updated.astype(BF16)


def gather_z(grid, low, parts):
    pieces = [low] + [grid.send(low, z=k) for k in range(1, grid.size["z"])]
    width = low.shape[1] // parts
    return [jnp.stack([p[:, s * width : (s + 1) * width] for p in pieces]) for s in range(parts)]


def gather_xy(grid, value, order):
    one_axis, two_axis = order
    pieces = [value] + [grid.send(value, **{two_axis: two}) for two in range(1, grid.size[two_axis])]
    value = jnp.stack(pieces)
    return [value] + [grid.send(value, **{one_axis: one}) for one in range(1, grid.size[one_axis])]


def project_kernel(grid, orders, rows, finish, tokens, *refs):
    refs = list(refs)
    size = grid.size
    pieces = [[[refs.pop(0) for _ in range(size[order[0]])] for order in orders] for _ in range(2)]
    gate = refs.pop(0) if finish else None
    out, held = refs
    width = out.shape[1] // len(orders)

    @pl.when(pl.program_id(0) == 0)
    def _():
        for kc in range(2):
            for kx in range(size["x"]):
                for ky in range(size["y"]):
                    for kz in range(size["z"]):
                        at = grid.here("x", -kx) * 2 + grid.here("c", kc)
                        at = (at * size["z"] + grid.here("z", -kz)) * size["y"] + grid.here("y", -ky)
                        start = pl.multiple_of(at * rows, rows)
                        for s, order in enumerate(orders):
                            one, two = (kx, ky) if order == "xy" else (ky, kx)
                            held[pl.ds(start, rows), s * width : (s + 1) * width] = pieces[kc][s][one][
                                two, kz
                            ].astype(held.dtype)

    value = jnp.dot(tokens[...], held[...].astype(BF16), preferred_element_type=F32)
    if finish:
        before = gate[...]
        value = before / (1.0 + jnp.exp(-before)) * value
    out[...] = value.astype(out.dtype)


def project(grid, tokens, pieces, orders, gate=None):
    count, depth = tokens.shape
    rows, width = pieces[0][0][0].shape[-2:]
    width *= len(orders)
    tile = min(count, 256)
    held = BF16 if rows % 16 == 0 else F32
    flat = [piece for core in pieces for part in core for piece in part]
    tiled = pl.BlockSpec((tile, width), lambda t: (t, 0))
    finish = gate is not None
    return pl.pallas_call(
        functools.partial(project_kernel, grid, orders, rows, finish),
        out_shape=jax.ShapeDtypeStruct((count, width), BF16 if finish else F32),
        grid=(count // tile,),
        in_specs=[pl.BlockSpec((tile, depth), lambda t: (t, 0))]
        + [pl.BlockSpec(memory_space=pltpu.VMEM)] * len(flat)
        + ([tiled] if finish else []),
        out_specs=tiled,
        scratch_shapes=[pltpu.VMEM((depth, width), held)],
        **kernel_params(2 * count * depth * width, count * depth * 2 + count * width * 8, SMALL),
    )(tokens, *flat, *([gate] if finish else []))


def shards(tokens, grad_out, master_weight, first_moment, second_moment, next_tokens):
    grid = Grid()
    half = grad_out.shape[1] // 2
    rows = master_weight.shape[0]
    lead = (grid.size["x"], grid.size["z"], grid.size["y"], rows, half)
    orders = ("xy", "yx")
    width = half // len(orders)

    sent = grad_rows(grid, tokens, grad_out, 1, BF16)
    came = [grid.send(value, c=1).reshape(lead) for value in sent]
    kept = [value.reshape(lead) for value in grad_rows(grid, tokens, grad_out, 0, F32)]

    def section(s):
        columns = slice(s * half, (s + 1) * half)
        ways = []
        for k, order in enumerate(orders):
            cut = slice(k * width, (k + 1) * width)
            ways.append(scatter_xy(grid, kept[s][..., cut], came[s][..., cut], order))
        for way in ways:
            next(way)
        yield
        for way in ways:
            next(way)
        yield
        way = scatter_z(grid, [next(way) for way in ways])
        next(way)
        yield
        grad = next(way)
        column_sums = sum_everywhere(grid, jnp.sum(grad * grad, axis=0).reshape(-1, 128))
        yield
        clipped = grad * clip_factor(jnp.sum(column_sums))
        state = [value[:, columns] for value in (master_weight, first_moment, second_moment)]
        low = adam(clipped, *state)
        low, clipped = lax.optimization_barrier((low, clipped))
        new = moments(clipped, *state[1:])
        values = gather_z(grid, low, len(orders))
        yield
        own = [gather_xy(grid, value, order) for value, order in zip(values, orders)]
        yield
        other = [[grid.send(piece, c=1) for piece in part] for part in own]
        yield new, (own, other)

    results = [None, None]
    ways = [section(0), section(1)]
    for step in range(7):
        for s in (0, 1):
            results[s] = next(ways[s])
    gate = project(grid, next_tokens, results[0][1], orders)
    next_hidden = project(grid, next_tokens, results[1][1], orders, gate)
    new_first, new_second = (jnp.concatenate([results[0][0][k], results[1][0][k]], axis=1) for k in (0, 1))
    return new_first, new_second, next_hidden


def solution(mesh):
    spec = P(AXES, None)
    return jax.shard_map(shards, mesh=mesh, in_specs=(spec,) * 6, out_specs=(spec,) * 3, check_vma=False)
```

```python
import functools
import math

import jax
import jax.numpy as jnp
from jax import lax
from jax.experimental import pallas as pl
from jax.experimental.pallas import tpu as pltpu
from jax.sharding import PartitionSpec as P

D = 2048
FF = 512
AXES = ("aa", "ba")
BF16 = jnp.bfloat16
F32 = jnp.float32
LARGE = 60 * 1024 * 1024
SMALL = 24 * 1024 * 1024


class Grid:
    def __init__(self):
        outer, inner = lax.axis_size("aa"), lax.axis_size("ba")
        y = 1
        while y * y * 4 <= inner:
            y *= 2
        self.size = {"x": outer // 2, "c": 2, "z": inner // y, "y": y}

    def here(self, axis, step=0):
        a, b = lax.axis_index("aa"), lax.axis_index("ba")
        inner = self.size["c"] if axis in "xc" else self.size["y"]
        index = a if axis in "xc" else b
        at = lax.div(index, inner) if axis in "xz" else lax.rem(index, inner)
        return lax.rem(at + step % self.size[axis], self.size[axis]) if step else at

    def send(self, value, **steps):
        pairs = []
        for x in range(self.size["x"]):
            for c in range(self.size["c"]):
                for z in range(self.size["z"]):
                    for y in range(self.size["y"]):
                        here = {"x": x, "c": c, "z": z, "y": y}
                        there = {k: (v + steps.get(k, 0)) % self.size[k] for k, v in here.items()}
                        pairs.append((self.index(here), self.index(there)))
        return lax.ppermute(value, AXES, pairs)

    def index(self, at):
        return ((at["x"] * self.size["c"] + at["c"]) * self.size["z"] + at["z"]) * self.size["y"] + at["y"]


def pick(value, axis, index):
    return lax.dynamic_index_in_dim(value, index, axis, keepdims=False)


def kernel_params(flops, moved, limit=LARGE):
    return dict(
        compiler_params=pltpu.CompilerParams(vmem_limit_bytes=limit),
        cost_estimate=pl.CostEstimate(flops=flops, bytes_accessed=moved, transcendentals=0),
    )


def column_block(grid, x, step, rows):
    return pl.ds(pl.multiple_of((x * 2 + grid.here("c", step)) * rows, rows), rows)


def product(block, cot):
    return lax.dot_general(block, cot, (((0,), (0,)), ((), ())), preferred_element_type=F32)


def sent_kernel(grid, tokens_ref, cot_ref, *refs):
    outs, (tokens, cot, sems) = refs[:-3], refs[-3:]
    n, _, rows = tokens.shape
    width = outs[0].shape[1]
    copies = [pltpu.make_async_copy(cot_ref, cot, sems.at[n])]
    for x in range(n):
        block = tokens_ref.at[:, column_block(grid, x, 1, rows)]
        copies.append(pltpu.make_async_copy(block, tokens.at[x], sems.at[x]))
    for copy in copies:
        copy.start()
    copies[0].wait()
    for x in range(n):
        copies[1 + x].wait()
        value = product(tokens[x], cot[...])
        for k, ref in enumerate(outs):
            ref[pl.ds(x * rows, rows), :] = value[:, k * width : (k + 1) * width].astype(ref.dtype)


def sent_rows(grid, tokens, cot, parts):
    count, depth = tokens.shape
    width = cot.shape[1] // parts
    n = grid.size["x"]
    rows = depth // (n * 2)
    return pl.pallas_call(
        functools.partial(sent_kernel, grid),
        out_shape=[jax.ShapeDtypeStruct((n * rows, width), BF16)] * parts,
        in_specs=[pl.BlockSpec(memory_space=pltpu.HBM)] * 2,
        out_specs=[pl.BlockSpec(memory_space=pltpu.VMEM)] * parts,
        scratch_shapes=[
            pltpu.VMEM((n, count, rows), BF16),
            pltpu.VMEM(cot.shape, BF16),
            pltpu.SemaphoreType.DMA((n + 1,)),
        ],
        **kernel_params(2 * count * n * rows * cot.shape[1], count * n * rows * 2 + cot.size * 2, SMALL),
    )(*(pltpu.with_memory_space_constraint(v, pltpu.HBM) for v in (tokens, cot)))


def kept_kernel(grid, orders, block_rows, tokens, cot, *refs):
    refs = list(refs)
    came = [refs.pop(0) for _ in orders]
    outs = [[refs.pop(0) for _ in range(grid.size[order[0]])] for order in orders]
    arrived, buffer, sems = refs
    nx, ny, nz = (grid.size[axis] for axis in "xyz")
    rows, width = buffer.shape
    copies = [pltpu.make_async_copy(ref, arrived.at[k], sems.at[k]) for k, ref in enumerate(came)]
    for copy in copies:
        copy.start()
    for kx in range(nx):
        x = grid.here("x", kx)
        value = product(tokens[:, column_block(grid, x, 0, rows)], cot[...])
        for k, order in enumerate(orders):
            if kx == 0:
                copies[k].wait()
            here = pl.ds(pl.multiple_of(x * rows, rows), rows)
            part = value[:, k * width : (k + 1) * width] + arrived[k, here, :].astype(F32)
            if order == "xy":
                outs[k][kx][...] = part.astype(outs[k][kx].dtype)
                continue
            buffer[...] = part
            for ky in range(ny):
                for z in range(nz):
                    start = pl.multiple_of((z * ny + grid.here("y", ky)) * block_rows, block_rows)
                    outs[k][ky][x, z] = buffer[pl.ds(start, block_rows), :].astype(outs[k][ky].dtype)


def kept_rows(grid, tokens, cot, came, orders):
    count, depth = tokens.shape
    width = cot.shape[1] // len(orders)
    nx, ny, nz = (grid.size[axis] for axis in "xyz")
    rows = depth // (nx * 2)
    block_rows = rows // (nz * ny)
    shapes = {"xy": (rows, width), "yx": (nx, nz, block_rows, width)}
    out_shape = [
        jax.ShapeDtypeStruct(shapes[order], BF16 if k else F32)
        for order in orders
        for k in range(grid.size[order[0]])
    ]
    whole = pl.BlockSpec(memory_space=pltpu.VMEM)
    outs = pl.pallas_call(
        functools.partial(kept_kernel, grid, orders, block_rows),
        out_shape=out_shape,
        in_specs=[whole] * 2 + [pl.BlockSpec(memory_space=pl.ANY)] * len(came),
        out_specs=[whole] * len(out_shape),
        scratch_shapes=[
            pltpu.VMEM((len(orders), nx * rows, width), BF16),
            pltpu.VMEM((rows, width), F32),
            pltpu.SemaphoreType.DMA((len(orders),)),
        ],
        **kernel_params(2 * count * nx * rows * cot.shape[1], count * nx * rows * 2 + cot.size * 2, SMALL),
    )(tokens, cot, *came)
    outs = iter(outs)
    result = []
    for order in orders:
        values = [next(outs) for _ in range(grid.size[order[0]])]
        result.append([v.reshape(nz, ny, block_rows, width) if order == "xy" else v for v in values])
    return result


def scatter_xy(grid, sums, order):
    one_axis, two_axis = order
    n_one, n_two = grid.size[one_axis], grid.size[two_axis]
    arriving = yield [(sums[one], {one_axis: one}) for one in range(1, n_one)]
    own = sums[0]
    for value in arriving:
        own = own + value.astype(F32)
    dim = 1 if two_axis == "y" else 0
    arriving = yield [
        (pick(own, dim, grid.here(two_axis, two)).astype(BF16), {two_axis: two}) for two in range(1, n_two)
    ]
    total = pick(own, dim, grid.here(two_axis))
    for value in arriving:
        total = total + value.astype(F32)
    yield total


def scatter_z(grid, totals):
    whole = jnp.concatenate(totals, axis=2)
    arriving = yield [
        (pick(whole, 0, grid.here("z", k)).astype(BF16), {"z": k}) for k in range(1, grid.size["z"])
    ]
    total = pick(whole, 0, grid.here("z"))
    for value in arriving:
        total = total + value.astype(F32)
    yield total


def sum_everywhere(grid, value):
    value = value + grid.send(value, c=1)
    plane = [(kx, ky) for kx in range(grid.size["x"]) for ky in range(grid.size["y"]) if kx + ky]
    value = sum([grid.send(value, x=kx, y=ky) for kx, ky in plane], value)
    return sum([grid.send(value, z=k) for k in range(1, grid.size["z"])], value)


def moments(clipped, first, second):
    return 0.9 * first + 0.1 * clipped, 0.95 * second + 0.05 * clipped * clipped


def clip_factor(square):
    return jnp.minimum(1.0, math.sqrt(D * FF) / jnp.sqrt(square + 1e-06))


def adam(clipped, weight, first, second):
    new_first, new_second = moments(clipped, first, second)
    corr_first = 1.0 - 0.9**10
    corr_second = 1.0 - 0.95**10
    updated = weight * (1.0 - 0.003 * 0.1) - 0.003 * (new_first / corr_first) / (
        jnp.sqrt(new_second / corr_second) + 1e-08
    )
    return updated.astype(BF16)


def gather_z(grid, low, parts):
    pieces = yield [(low, {"z": k}) for k in range(1, grid.size["z"])]
    width = low.shape[1] // parts
    yield [jnp.stack([p[:, s * width : (s + 1) * width] for p in [low] + pieces]) for s in range(parts)]


def gather_xy(grid, value, order):
    one_axis, two_axis = order
    pieces = yield [(value, {two_axis: two}) for two in range(1, grid.size[two_axis])]
    value = jnp.stack([value] + pieces)
    pieces = yield [(value, {one_axis: one}) for one in range(1, grid.size[one_axis])]
    yield [value] + pieces


def stage(grid, wanted, after=()):
    values = [value for sends in wanted for value, _ in sends]
    if after:
        values, _ = lax.optimization_barrier((values, tuple(after)))
    flat = iter(values)
    return [[grid.send(next(flat), **steps) for _, steps in sends] for sends in wanted], values


def project_kernel(grid, orders, rows, finish, tokens, *refs):
    refs = list(refs)
    size = grid.size
    pieces = [[[refs.pop(0) for _ in range(size[order[0]])] for order in orders] for _ in range(2)]
    gate = refs.pop(0) if finish else None
    out, held = refs
    width = out.shape[1] // len(orders)

    @pl.when(pl.program_id(0) == 0)
    def _():
        for kc in range(2):
            for kx in range(size["x"]):
                for ky in range(size["y"]):
                    for kz in range(size["z"]):
                        at = grid.here("x", -kx) * 2 + grid.here("c", kc)
                        at = (at * size["z"] + grid.here("z", -kz)) * size["y"] + grid.here("y", -ky)
                        start = pl.multiple_of(at * rows, rows)
                        for s, order in enumerate(orders):
                            one, two = (kx, ky) if order == "xy" else (ky, kx)
                            held[pl.ds(start, rows), s * width : (s + 1) * width] = pieces[kc][s][one][
                                two, kz
                            ].astype(held.dtype)

    value = jnp.dot(tokens[...], held[...].astype(BF16), preferred_element_type=F32)
    if finish:
        before = gate[...]
        value = before / (1.0 + jnp.exp(-before)) * value
    out[...] = value.astype(out.dtype)


def project(grid, tokens, pieces, orders, gate=None):
    count, depth = tokens.shape
    rows, width = pieces[0][0][0].shape[-2:]
    width *= len(orders)
    tile = min(count, 256)
    held = BF16 if rows % 16 == 0 else F32
    flat = [piece for core in pieces for part in core for piece in part]
    tiled = pl.BlockSpec((tile, width), lambda t: (t, 0))
    finish = gate is not None
    return pl.pallas_call(
        functools.partial(project_kernel, grid, orders, rows, finish),
        out_shape=jax.ShapeDtypeStruct((count, width), BF16 if finish else F32),
        grid=(count // tile,),
        in_specs=[pl.BlockSpec((tile, depth), lambda t: (t, 0))]
        + [pl.BlockSpec(memory_space=pltpu.VMEM)] * len(flat)
        + ([tiled] if finish else []),
        out_specs=tiled,
        scratch_shapes=[pltpu.VMEM((depth, width), held)],
        **kernel_params(2 * count * depth * width, count * depth * 2 + count * width * 8, SMALL),
    )(tokens, *flat, *([gate] if finish else []))


def shards(tokens, grad_out, master_weight, first_moment, second_moment, next_tokens):
    grid = Grid()
    half = grad_out.shape[1] // 2
    orders = ("xy", "yx")

    came = [grid.send(value, c=1) for value in sent_rows(grid, tokens, grad_out, 2 * len(orders))]
    sums = kept_rows(grid, tokens, grad_out, came, 2 * orders)

    def section(s):
        columns = slice(s * half, (s + 1) * half)
        first = s * len(orders)
        ways = [scatter_xy(grid, sums[first + k], order) for k, order in enumerate(orders)]
        wanted = [next(way) for way in ways]
        for _ in range(2):
            came_in, values = stage(grid, wanted, (yield))
            yield values
            wanted = [way.send(got) for way, got in zip(ways, came_in)]
        way = scatter_z(grid, wanted)
        (came_in,), values = stage(grid, [next(way)], (yield))
        yield values
        grad = way.send(came_in)
        square = yield jnp.sum(grad * grad, axis=0).reshape(-1, 128)
        clipped = grad * clip_factor(square)
        state = [value[:, columns] for value in (master_weight, first_moment, second_moment)]
        low = adam(clipped, *state)
        low, clipped = lax.optimization_barrier((low, clipped))
        new = moments(clipped, *state[1:])
        way = gather_z(grid, low, len(orders))
        yield
        (came_in,), values = stage(grid, [next(way)], (yield))
        yield values
        ways = [gather_xy(grid, value, order) for value, order in zip(way.send(came_in), orders)]
        wanted = [next(way) for way in ways]
        for _ in range(2):
            came_in, values = stage(grid, wanted, (yield))
            yield values
            wanted = [way.send(got) for way, got in zip(ways, came_in)]
        own = wanted
        early = [[grid.send(part[0], c=1)] for part in own]
        after = yield new
        last, _ = stage(grid, [[(piece, {"c": 1}) for piece in part[1:]] for part in own], after)
        other = [a + b for a, b in zip(early, last)]
        yield own, other

    ways = [section(0), section(1)]

    def run(stages):
        for _ in range(stages):
            for way in ways:
                next(way)
                way.send(())

    run(3)
    squares = [next(way) for way in ways]
    squares = sum_everywhere(grid, jnp.stack(squares))
    for s in (0, 1):
        ways[s].send(jnp.sum(squares[s]))
    run(3)
    news = [next(way) for way in ways]
    gate = project(grid, next_tokens, ways[0].send([]), orders)
    next_hidden = project(grid, next_tokens, ways[1].send([gate]), orders, gate)
    new_first, new_second = (jnp.concatenate([news[0][k], news[1][k]], axis=1) for k in (0, 1))
    return new_first, new_second, next_hidden


def solution(mesh):
    spec = P(AXES, None)
    return jax.shard_map(shards, mesh=mesh, in_specs=(spec,) * 6, out_specs=(spec,) * 3, check_vma=False)
```

```python
import functools
import math

import jax
import jax.numpy as jnp
from jax import lax
from jax.experimental import pallas as pl
from jax.experimental.pallas import tpu as pltpu
from jax.sharding import PartitionSpec as P

D = 2048
FF = 512
AXES = ("aa", "ba")
BF16 = jnp.bfloat16
F32 = jnp.float32
LANES = 128
LARGE = 60 * 1024 * 1024
SMALL = 24 * 1024 * 1024


class Grid:
    def __init__(self):
        outer, inner = lax.axis_size("aa"), lax.axis_size("ba")
        y = 1
        while y * y * 4 <= inner:
            y *= 2
        self.size = {"x": outer // 2, "c": 2, "z": inner // y, "y": y}

    def here(self, axis, step=0):
        a, b = lax.axis_index("aa"), lax.axis_index("ba")
        inner = self.size["c"] if axis in "xc" else self.size["y"]
        index = a if axis in "xc" else b
        return self.partner(axis, lax.div(index, inner) if axis in "xz" else lax.rem(index, inner), step)

    def partner(self, axis, at, step):
        return at ^ step if step else at

    def send(self, value, **steps):
        pairs = []
        for x in range(self.size["x"]):
            for c in range(self.size["c"]):
                for z in range(self.size["z"]):
                    for y in range(self.size["y"]):
                        here = {"x": x, "c": c, "z": z, "y": y}
                        there = {k: int(self.partner(k, v, steps.get(k, 0))) for k, v in here.items()}
                        pairs.append((self.index(here), self.index(there)))
        return lax.ppermute(value, AXES, pairs)

    def index(self, at):
        return ((at["x"] * self.size["c"] + at["c"]) * self.size["z"] + at["z"]) * self.size["y"] + at["y"]


def pick(value, axis, index):
    return lax.dynamic_index_in_dim(value, index, axis, keepdims=False)


def kernel_params(flops, moved, limit=LARGE):
    return dict(
        compiler_params=pltpu.CompilerParams(vmem_limit_bytes=limit),
        cost_estimate=pl.CostEstimate(flops=flops, bytes_accessed=moved, transcendentals=0),
    )


def column_block(grid, x, step, rows):
    return pl.ds(pl.multiple_of((x * 2 + grid.here("c", step)) * rows, rows), rows)


def product(block, cot):
    return lax.dot_general(block, cot, (((0,), (0,)), ((), ())), preferred_element_type=F32)


def sent_kernel(grid, tokens_ref, cot_ref, *refs):
    outs, (tokens, cot, sems) = refs[:-3], refs[-3:]
    n, _, rows = tokens.shape
    width = outs[0].shape[1]
    copies = [pltpu.make_async_copy(cot_ref, cot, sems.at[n])]
    for x in range(n):
        block = tokens_ref.at[:, column_block(grid, x, 1, rows)]
        copies.append(pltpu.make_async_copy(block, tokens.at[x], sems.at[x]))
    for copy in copies:
        copy.start()
    copies[0].wait()
    for x in range(n):
        copies[1 + x].wait()
        value = product(tokens[x], cot[...])
        for k, ref in enumerate(outs):
            ref[pl.ds(x * rows, rows), :] = value[:, k * width : (k + 1) * width].astype(ref.dtype)


def sent_rows(grid, tokens, cot, parts):
    count, depth = tokens.shape
    width = cot.shape[1] // parts
    n = grid.size["x"]
    rows = depth // (n * 2)
    return pl.pallas_call(
        functools.partial(sent_kernel, grid),
        out_shape=[jax.ShapeDtypeStruct((n * rows, width), BF16)] * parts,
        in_specs=[pl.BlockSpec(memory_space=pltpu.HBM)] * 2,
        out_specs=[pl.BlockSpec(memory_space=pltpu.VMEM)] * parts,
        scratch_shapes=[
            pltpu.VMEM((n, count, rows), BF16),
            pltpu.VMEM(cot.shape, BF16),
            pltpu.SemaphoreType.DMA((n + 1,)),
        ],
        **kernel_params(2 * count * n * rows * cot.shape[1], count * n * rows * 2 + cot.size * 2, SMALL),
    )(*(pltpu.with_memory_space_constraint(v, pltpu.HBM) for v in (tokens, cot)))


def kept_kernel(grid, orders, block_rows, tokens, cot, *refs):
    refs = list(refs)
    came = [refs.pop(0) for _ in orders]
    outs = [[refs.pop(0) for _ in range(grid.size[order[0]])] for order in orders]
    arrived, buffer, sems = refs
    nx, ny, nz = (grid.size[axis] for axis in "xyz")
    rows, width = buffer.shape
    copies = [pltpu.make_async_copy(ref, arrived.at[k], sems.at[k]) for k, ref in enumerate(came)]
    for copy in copies:
        copy.start()
    for kx in range(nx):
        x = grid.here("x", kx)
        value = product(tokens[:, column_block(grid, x, 0, rows)], cot[...])
        for k, order in enumerate(orders):
            if kx == 0:
                copies[k].wait()
            here = pl.ds(pl.multiple_of(x * rows, rows), rows)
            part = value[:, k * width : (k + 1) * width] + arrived[k, here, :].astype(F32)
            if order == "xy":
                outs[k][kx][...] = part.astype(outs[k][kx].dtype)
                continue
            buffer[...] = part
            for ky in range(ny):
                for z in range(nz):
                    start = pl.multiple_of((z * ny + grid.here("y", ky)) * block_rows, block_rows)
                    outs[k][ky][x, z] = buffer[pl.ds(start, block_rows), :].astype(outs[k][ky].dtype)


def kept_rows(grid, tokens, cot, came, orders):
    count, depth = tokens.shape
    width = cot.shape[1] // len(orders)
    nx, ny, nz = (grid.size[axis] for axis in "xyz")
    rows = depth // (nx * 2)
    block_rows = rows // (nz * ny)
    shapes = {"xy": (rows, width), "yx": (nx, nz, block_rows, width)}
    out_shape = [
        jax.ShapeDtypeStruct(shapes[order], BF16 if k else F32)
        for order in orders
        for k in range(grid.size[order[0]])
    ]
    whole = pl.BlockSpec(memory_space=pltpu.VMEM)
    outs = pl.pallas_call(
        functools.partial(kept_kernel, grid, orders, block_rows),
        out_shape=out_shape,
        in_specs=[whole] * 2 + [pl.BlockSpec(memory_space=pl.ANY)] * len(came),
        out_specs=[whole] * len(out_shape),
        scratch_shapes=[
            pltpu.VMEM((len(orders), nx * rows, width), BF16),
            pltpu.VMEM((rows, width), F32),
            pltpu.SemaphoreType.DMA((len(orders),)),
        ],
        **kernel_params(2 * count * nx * rows * cot.shape[1], count * nx * rows * 2 + cot.size * 2, SMALL),
    )(tokens, cot, *came)
    outs = iter(outs)
    result = []
    for order in orders:
        values = [next(outs) for _ in range(grid.size[order[0]])]
        result.append([v.reshape(nz, ny, block_rows, width) if order == "xy" else v for v in values])
    return result


def scatter_xy(grid, sums, order):
    one_axis, two_axis = order
    n_one, n_two = grid.size[one_axis], grid.size[two_axis]
    arriving = yield [(sums[one], {one_axis: one}) for one in range(1, n_one)]
    own = sums[0]
    for value in arriving:
        own = own + value.astype(F32)
    dim = 1 if two_axis == "y" else 0
    arriving = yield [
        (pick(own, dim, grid.here(two_axis, two)).astype(BF16), {two_axis: two}) for two in range(1, n_two)
    ]
    total = pick(own, dim, grid.here(two_axis))
    for value in arriving:
        total = total + value.astype(F32)
    yield total


def scatter_z(grid, totals):
    whole = jnp.concatenate(totals, axis=2)
    arriving = yield [
        (pick(whole, 0, grid.here("z", k)).astype(BF16), {"z": k}) for k in range(1, grid.size["z"])
    ]
    total = pick(whole, 0, grid.here("z"))
    for value in arriving:
        total = total + value.astype(F32)
    yield total


def sum_everywhere(value):
    count = lax.axis_size("aa") * lax.axis_size("ba")
    terms = lax.all_to_all(jnp.broadcast_to(value, (count, *value.shape)), AXES, 0, 0, tiled=True)
    return jnp.sum(terms, axis=(0, 2))


def moments(clipped, first, second):
    return 0.9 * first + 0.1 * clipped, 0.95 * second + 0.05 * clipped * clipped


def clip_factor(square):
    return jnp.minimum(1.0, math.sqrt(D * FF) / jnp.sqrt(square + 1e-06))


def adam(clipped, weight, first, second):
    new_first, new_second = moments(clipped, first, second)
    corr_first = 1.0 - 0.9**10
    corr_second = 1.0 - 0.95**10
    updated = weight * (1.0 - 0.003 * 0.1) - 0.003 * (new_first / corr_first) / (
        jnp.sqrt(new_second / corr_second) + 1e-08
    )
    return updated.astype(BF16)


def gather_z(grid, low, parts):
    pieces = yield [(low, {"z": k}) for k in range(1, grid.size["z"])]
    width = low.shape[1] // parts
    yield [jnp.stack([p[:, s * width : (s + 1) * width] for p in [low] + pieces]) for s in range(parts)]


def gather_xy(grid, value, order):
    one_axis, two_axis = order
    pieces = yield [(value, {two_axis: two}) for two in range(1, grid.size[two_axis])]
    value = jnp.stack([value] + pieces)
    pieces = yield [(value, {one_axis: one}) for one in range(1, grid.size[one_axis])]
    yield [value] + pieces


def stage(grid, wanted, after=()):
    values = [value for sends in wanted for value, _ in sends]
    if after:
        values, _ = lax.optimization_barrier((values, tuple(after)))
    flat = iter(values)
    return [[grid.send(next(flat), **steps) for _, steps in sends] for sends in wanted], values


def project_kernel(grid, orders, rows, halves, finish, *refs):
    refs = list(refs)
    nx, ny, nz = (grid.size[axis] for axis in "xyz")
    tokens = refs.pop(0)
    places = [(h, kc) for h, half in enumerate(halves) for kc in half]
    pieces = [[[refs.pop(0) for _ in range(grid.size[order[0]])] for order in orders] for _ in places]
    earlier = refs.pop(0) if finish else None
    out, held = refs
    width = out.shape[1] // len(orders)
    block = nz * ny * rows

    @pl.when(pl.program_id(0) == 0)
    def _():
        for i in range(len(places)):
            for kx in range(nx):
                for ky in range(ny):
                    for kz in range(nz):
                        at = (grid.here("x", kx) * nz + grid.here("z", kz)) * ny + grid.here("y", ky)
                        start = pl.multiple_of(at * rows, rows)
                        for s, order in enumerate(orders):
                            one, two = (kx, ky) if order == "xy" else (ky, kx)
                            held[i, pl.ds(start, rows), s * width : (s + 1) * width] = pieces[i][s][one][
                                two, kz
                            ].astype(held.dtype)

    tile = pl.ds(pl.multiple_of(pl.program_id(0) * out.shape[0], out.shape[0]), out.shape[0])
    totals = [earlier[tile, :], None] if finish else [None]
    for i, (h, kc) in enumerate(places):
        for x in range(nx):
            weight = held[i, x * block : (x + 1) * block, :].astype(BF16)
            term = jnp.dot(tokens[tile, column_block(grid, x, kc, block)], weight, preferred_element_type=F32)
            totals[h] = term if totals[h] is None else totals[h] + term
    value = totals[0]
    if finish:
        value = value / (1.0 + jnp.exp(-value)) * totals[1]
    out[...] = value.astype(out.dtype)


def project(grid, tokens, halves, orders, earlier=None):
    count, depth = tokens.shape
    nx = grid.size["x"]
    block = depth // (nx * 2)
    flat = [piece for half in halves for table in half.values() for part in table for piece in part]
    rows, width = flat[0].shape[-2:]
    width *= len(orders)
    tile = min(count, 512)
    held = BF16 if rows % 16 == 0 else F32
    finish = earlier is not None
    keys = [tuple(half) for half in halves]

    tiled = pl.BlockSpec((tile, width), lambda t: (t, 0))
    places = sum(len(key) for key in keys)
    return pl.pallas_call(
        functools.partial(project_kernel, grid, orders, rows, keys, finish),
        out_shape=jax.ShapeDtypeStruct((count, width), BF16 if finish else F32),
        grid=(count // tile,),
        in_specs=[pl.BlockSpec(memory_space=pltpu.VMEM)] * (1 + len(flat) + finish),
        out_specs=tiled,
        scratch_shapes=[pltpu.VMEM((places, nx * block, width), held)],
        **kernel_params(
            2 * count * nx * block * places * width, count * depth * 2 + count * width * 8, SMALL
        ),
    )(tokens, *flat, *([earlier] if finish else []))


def shards(tokens, grad_out, master_weight, first_moment, second_moment, next_tokens):
    grid = Grid()
    half = grad_out.shape[1] // 2
    orders = ("xy", "yx")

    came = [grid.send(value, c=1) for value in sent_rows(grid, tokens, grad_out, 2 * len(orders))]
    sums = kept_rows(grid, tokens, grad_out, came, 2 * orders)

    def section(s):
        columns = slice(s * half, (s + 1) * half)
        first = s * len(orders)
        ways = [scatter_xy(grid, sums[first + k], order) for k, order in enumerate(orders)]
        wanted = [next(way) for way in ways]
        for _ in range(2):
            came_in, values = stage(grid, wanted, (yield))
            yield values
            wanted = [way.send(got) for way, got in zip(ways, came_in)]
        way = scatter_z(grid, wanted)
        (came_in,), values = stage(grid, [next(way)], (yield))
        yield values
        grad = way.send(came_in)
        factor = yield jnp.sum((grad * grad).reshape(grad.shape[0], -1, LANES), axis=(0, 1))
        clipped = grad * factor
        state = [value[:, columns] for value in (master_weight, first_moment, second_moment)]
        low = adam(clipped, *state)
        low, clipped = lax.optimization_barrier((low, clipped))
        new = moments(clipped, *state[1:])
        way = gather_z(grid, low, len(orders))
        yield
        (came_in,), values = stage(grid, [next(way)], (yield))
        yield values
        ways = [gather_xy(grid, value, order) for value, order in zip(way.send(came_in), orders)]
        wanted = [next(way) for way in ways]
        for _ in range(2):
            came_in, values = stage(grid, wanted, (yield))
            yield values
            wanted = [way.send(got) for way, got in zip(ways, came_in)]
        own = wanted
        early = [[grid.send(part[0], c=1)] for part in own]
        after = yield new, own
        last, _ = stage(grid, [[(piece, {"c": 1}) for piece in part[1:]] for part in own], after)
        other = [a + b for a, b in zip(early, last)]
        yield other

    ways = [section(0), section(1)]

    def run(stages):
        for _ in range(stages):
            for way in ways:
                next(way)
                way.send(())

    run(3)
    squares = [next(way) for way in ways]
    factors = clip_factor(sum_everywhere(jnp.stack(squares)))
    factors = lax.optimization_barrier(jnp.broadcast_to(factors[:, None, None], (2, 1, half)))
    for s in (0, 1):
        ways[s].send(factors[s])
    run(3)
    news, own = zip(*[next(way) for way in ways])
    new = [jnp.concatenate([news[0][k], news[1][k]], axis=1) for k in (0, 1)]
    gate = project(grid, next_tokens, [{0: own[0]}], orders)
    other = [ways[0].send([]), ways[1].send([gate])]
    halves = [{1: other[0]}, {0: own[1], 1: other[1]}]
    return *new, project(grid, next_tokens, halves, orders, gate)


def solution(mesh):
    spec = P(AXES, None)
    return jax.shard_map(shards, mesh=mesh, in_specs=(spec,) * 6, out_specs=(spec,) * 3, check_vma=False)
```

```python
import functools
import math

import jax
import jax.numpy as jnp
from jax import lax
from jax.experimental import pallas as pl
from jax.experimental.pallas import tpu as pltpu
from jax.sharding import PartitionSpec as P

D = 2048
FF = 512
AXES = ("aa", "ba")
BF16 = jnp.bfloat16
F32 = jnp.float32
LANES = 128
LARGE = 60 * 1024 * 1024
SMALL = 24 * 1024 * 1024


class Grid:
    def __init__(self):
        outer, inner = lax.axis_size("aa"), lax.axis_size("ba")
        y = 1
        while y * y * 4 <= inner:
            y *= 2
        self.size = {"x": outer // 2, "c": 2, "z": inner // y, "y": y}

    def here(self, axis, step=0):
        a, b = lax.axis_index("aa"), lax.axis_index("ba")
        inner = self.size["c"] if axis in "xc" else self.size["y"]
        index = a if axis in "xc" else b
        return self.partner(axis, lax.div(index, inner) if axis in "xz" else lax.rem(index, inner), step)

    def partner(self, axis, at, step):
        return at ^ step if step else at

    def send(self, value, **steps):
        pairs = []
        for x in range(self.size["x"]):
            for c in range(self.size["c"]):
                for z in range(self.size["z"]):
                    for y in range(self.size["y"]):
                        here = {"x": x, "c": c, "z": z, "y": y}
                        there = {k: int(self.partner(k, v, steps.get(k, 0))) for k, v in here.items()}
                        pairs.append((self.index(here), self.index(there)))
        return lax.ppermute(value, AXES, pairs)

    def index(self, at):
        return ((at["x"] * self.size["c"] + at["c"]) * self.size["z"] + at["z"]) * self.size["y"] + at["y"]


def pick(value, axis, index):
    return lax.dynamic_index_in_dim(value, index, axis, keepdims=False)


def kernel_params(flops, moved, limit=LARGE):
    return dict(
        compiler_params=pltpu.CompilerParams(vmem_limit_bytes=limit),
        cost_estimate=pl.CostEstimate(flops=flops, bytes_accessed=moved, transcendentals=0),
    )


def column_block(grid, x, step, rows):
    return pl.ds(pl.multiple_of((x * 2 + grid.here("c", step)) * rows, rows), rows)


def product(block, cot):
    return lax.dot_general(block, cot, (((0,), (0,)), ((), ())), preferred_element_type=F32)


def sent_kernel(grid, tokens_ref, cot_ref, *refs):
    outs, (tokens, cot, sems) = refs[:-3], refs[-3:]
    n, _, rows = tokens.shape
    width = outs[0].shape[1]
    copies = [pltpu.make_async_copy(cot_ref, cot, sems.at[n])]
    for x in range(n):
        block = tokens_ref.at[:, column_block(grid, x, 1, rows)]
        copies.append(pltpu.make_async_copy(block, tokens.at[x], sems.at[x]))
    for copy in copies:
        copy.start()
    copies[0].wait()
    for x in range(n):
        copies[1 + x].wait()
        value = product(tokens[x], cot[...])
        for k, ref in enumerate(outs):
            ref[pl.ds(x * rows, rows), :] = value[:, k * width : (k + 1) * width].astype(ref.dtype)


def sent_rows(grid, tokens, cot, parts):
    count, depth = tokens.shape
    width = cot.shape[1] // parts
    n = grid.size["x"]
    rows = depth // (n * 2)
    return pl.pallas_call(
        functools.partial(sent_kernel, grid),
        out_shape=[jax.ShapeDtypeStruct((n * rows, width), BF16)] * parts,
        in_specs=[pl.BlockSpec(memory_space=pltpu.HBM)] * 2,
        out_specs=[pl.BlockSpec(memory_space=pltpu.VMEM)] * parts,
        scratch_shapes=[
            pltpu.VMEM((n, count, rows), BF16),
            pltpu.VMEM(cot.shape, BF16),
            pltpu.SemaphoreType.DMA((n + 1,)),
        ],
        **kernel_params(2 * count * n * rows * cot.shape[1], count * n * rows * 2 + cot.size * 2, SMALL),
    )(*(pltpu.with_memory_space_constraint(v, pltpu.HBM) for v in (tokens, cot)))


def kept_kernel(grid, orders, block_rows, tokens, cot, *refs):
    refs = list(refs)
    came = [refs.pop(0) for _ in orders]
    outs = [[refs.pop(0) for _ in range(grid.size[order[0]])] for order in orders]
    arrived, buffer, sems = refs
    nx, ny, nz = (grid.size[axis] for axis in "xyz")
    rows, width = buffer.shape
    copies = [pltpu.make_async_copy(ref, arrived.at[k], sems.at[k]) for k, ref in enumerate(came)]
    for copy in copies:
        copy.start()
    for kx in range(nx):
        x = grid.here("x", kx)
        value = product(tokens[:, column_block(grid, x, 0, rows)], cot[...])
        for k, order in enumerate(orders):
            if kx == 0:
                copies[k].wait()
            here = pl.ds(pl.multiple_of(x * rows, rows), rows)
            part = value[:, k * width : (k + 1) * width] + arrived[k, here, :].astype(F32)
            buffer[...] = part
            for y in range(ny):
                out, at = (outs[k][kx], y) if order == "xy" else (outs[k][y], x)
                near = y if order == "xy" else grid.here("y", y)
                for z in range(nz):
                    start = pl.multiple_of((z * ny + near) * block_rows, block_rows)
                    out[at, z] = buffer[pl.ds(start, block_rows), :].astype(out.dtype)


def kept_rows(grid, tokens, cot, came, orders):
    count, depth = tokens.shape
    width = cot.shape[1] // len(orders)
    nx, ny, nz = (grid.size[axis] for axis in "xyz")
    rows = depth // (nx * 2)
    block_rows = rows // (nz * ny)
    shapes = {"xy": (ny, nz, block_rows, width), "yx": (nx, nz, block_rows, width)}
    out_shape = [
        jax.ShapeDtypeStruct(shapes[order], BF16 if k else F32)
        for order in orders
        for k in range(grid.size[order[0]])
    ]
    whole = pl.BlockSpec(memory_space=pltpu.VMEM)
    outs = pl.pallas_call(
        functools.partial(kept_kernel, grid, orders, block_rows),
        out_shape=out_shape,
        in_specs=[whole] * 2 + [pl.BlockSpec(memory_space=pl.ANY)] * len(came),
        out_specs=[whole] * len(out_shape),
        scratch_shapes=[
            pltpu.VMEM((len(orders), nx * rows, width), BF16),
            pltpu.VMEM((rows, width), F32),
            pltpu.SemaphoreType.DMA((len(orders),)),
        ],
        **kernel_params(2 * count * nx * rows * cot.shape[1], count * nx * rows * 2 + cot.size * 2, SMALL),
    )(tokens, cot, *came)
    outs = iter(outs)
    result = []
    for order in orders:
        values = [next(outs) for _ in range(grid.size[order[0]])]
        result.append(values)
    return result


def scatter_xy(grid, sums, order):
    one_axis, two_axis = order
    n_one, n_two = grid.size[one_axis], grid.size[two_axis]
    arriving = yield [(sums[one], {one_axis: one}) for one in range(1, n_one)]
    own = sums[0]
    for value in arriving:
        own = own + value.astype(F32)
    arriving = yield [
        (pick(own, 0, grid.here(two_axis, two)).astype(BF16), {two_axis: two}) for two in range(1, n_two)
    ]
    total = pick(own, 0, grid.here(two_axis))
    for value in arriving:
        total = total + value.astype(F32)
    yield total


def scatter_z(grid, totals):
    whole = jnp.concatenate(totals, axis=2)
    arriving = yield [
        (pick(whole, 0, grid.here("z", k)).astype(BF16), {"z": k}) for k in reversed(range(1, grid.size["z"]))
    ]
    total = pick(whole, 0, grid.here("z"))
    for value in arriving:
        total = total + value.astype(F32)
    yield total


def sum_everywhere(value):
    count = lax.axis_size("aa") * lax.axis_size("ba")
    terms = lax.all_to_all(jnp.broadcast_to(value, (count, *value.shape)), AXES, 0, 0, tiled=True)
    return jnp.sum(terms, axis=(0, 2))


def moments(clipped, first, second):
    return 0.9 * first + 0.1 * clipped, 0.95 * second + 0.05 * clipped * clipped


def clip_factor(square):
    return jnp.minimum(1.0, math.sqrt(D * FF) / jnp.sqrt(square + 1e-06))


def adam(clipped, weight, first, second):
    new_first, new_second = moments(clipped, first, second)
    corr_first = 1.0 - 0.9**10
    corr_second = 1.0 - 0.95**10
    updated = weight * (1.0 - 0.003 * 0.1) - 0.003 * (new_first / corr_first) / (
        jnp.sqrt(new_second / corr_second) + 1e-08
    )
    return updated.astype(BF16)


def gather_z(grid, low, parts):
    pieces = yield [(low, {"z": k}) for k in reversed(range(1, grid.size["z"]))]
    width = low.shape[1] // parts
    yield [jnp.stack([p[:, s * width : (s + 1) * width] for p in [low] + pieces[::-1]]) for s in range(parts)]


def gather_xy(grid, value, order):
    one_axis, two_axis = order
    pieces = yield [(value, {two_axis: two}) for two in range(1, grid.size[two_axis])]
    value = jnp.stack([value] + pieces)
    pieces = yield [(value, {one_axis: one}) for one in range(1, grid.size[one_axis])]
    yield [value] + pieces


def stage(grid, wanted, after=()):
    values = [value for sends in wanted for value, _ in sends]
    if after:
        values, _ = lax.optimization_barrier((values, tuple(after)))
    flat = iter(values)
    return [[grid.send(next(flat), **steps) for _, steps in sends] for sends in wanted], values


def project_kernel(grid, orders, rows, halves, finish, *refs):
    refs = list(refs)
    nx, ny, nz = (grid.size[axis] for axis in "xyz")
    tokens = refs.pop(0)
    places = [(h, kc) for h, half in enumerate(halves) for kc in half]
    pieces = [[[refs.pop(0) for _ in range(grid.size[order[0]])] for order in orders] for _ in places]
    if finish:
        earlier, *state = [refs.pop(0) for _ in range(5)]
        out, *new, held = refs
    else:
        out, held = refs
    width = out.shape[1] // len(orders)
    block = nz * ny * rows

    @pl.when(pl.program_id(0) == 0)
    def _():
        if finish:
            *clipped, first, second = state
            for s, ref in enumerate(clipped):
                at = slice(s * ref.shape[1], (s + 1) * ref.shape[1])
                new[0][:, at], new[1][:, at] = moments(ref[...], first[:, at], second[:, at])
        for i in range(len(places)):
            for kx in range(nx):
                for ky in range(ny):
                    for kz in range(nz):
                        at = (grid.here("x", kx) * nz + grid.here("z", kz)) * ny + grid.here("y", ky)
                        start = pl.multiple_of(at * rows, rows)
                        for s, order in enumerate(orders):
                            one, two = (kx, ky) if order == "xy" else (ky, kx)
                            held[i, pl.ds(start, rows), s * width : (s + 1) * width] = pieces[i][s][one][
                                two, kz
                            ].astype(held.dtype)

    tile = pl.ds(pl.multiple_of(pl.program_id(0) * out.shape[0], out.shape[0]), out.shape[0])
    totals = [earlier[tile, :], None] if finish else [None]
    for i, (h, kc) in enumerate(places):
        for x in range(nx):
            weight = held[i, x * block : (x + 1) * block, :].astype(BF16)
            term = jnp.dot(tokens[tile, column_block(grid, x, kc, block)], weight, preferred_element_type=F32)
            totals[h] = term if totals[h] is None else totals[h] + term
    value = totals[0]
    if finish:
        value = value / (1.0 + jnp.exp(-value)) * totals[1]
    out[...] = value.astype(out.dtype)


def project(grid, tokens, halves, orders, earlier=None, state=()):
    count, depth = tokens.shape
    nx = grid.size["x"]
    block = depth // (nx * 2)
    flat = [piece for half in halves for table in half.values() for part in table for piece in part]
    rows, width = flat[0].shape[-2:]
    width *= len(orders)
    tile = min(count, 512)
    held = BF16 if rows % 16 == 0 else F32
    finish = earlier is not None
    keys = [tuple(half) for half in halves]

    tiled = pl.BlockSpec((tile, width), lambda t: (t, 0))
    places = sum(len(key) for key in keys)
    return pl.pallas_call(
        functools.partial(project_kernel, grid, orders, rows, keys, finish),
        out_shape=[jax.ShapeDtypeStruct((count, width), BF16 if finish else F32)]
        + [jax.ShapeDtypeStruct(value.shape, F32) for value in state[-2:]],
        grid=(count // tile,),
        in_specs=[pl.BlockSpec(memory_space=pltpu.VMEM)] * (1 + len(flat) + finish + len(state)),
        out_specs=[tiled] + [pl.BlockSpec(value.shape, lambda t: (0, 0)) for value in state[-2:]],
        scratch_shapes=[pltpu.VMEM((places, nx * block, width), held)],
        **kernel_params(
            2 * count * nx * block * places * width, count * depth * 2 + count * width * 8, SMALL
        ),
    )(tokens, *flat, *([earlier] if finish else []), *state)


def shards(tokens, grad_out, master_weight, first_moment, second_moment, next_tokens):
    grid = Grid()
    half = grad_out.shape[1] // 2
    orders = ("xy", "yx")

    came = [grid.send(value, c=1) for value in sent_rows(grid, tokens, grad_out, 2 * len(orders))]
    sums = kept_rows(grid, tokens, grad_out, came, 2 * orders)

    def section(s):
        columns = slice(s * half, (s + 1) * half)
        first = s * len(orders)
        ways = [scatter_xy(grid, sums[first + k], order) for k, order in enumerate(orders)]
        wanted = [next(way) for way in ways]
        for _ in range(2):
            came_in, values = stage(grid, wanted, (yield))
            came_in = lax.optimization_barrier(came_in)
            yield values
            wanted = [way.send(got) for way, got in zip(ways, came_in)]
        way = scatter_z(grid, wanted)
        (came_in,), values = stage(grid, [next(way)], (yield))
        yield values
        grad = way.send(came_in)
        factor = yield jnp.sum((grad * grad).reshape(grad.shape[0], -1, LANES), axis=(0, 1))
        clipped = grad * factor
        state = [value[:, columns] for value in (master_weight, first_moment, second_moment)]
        low = adam(clipped, *state)
        low, clipped = lax.optimization_barrier((low, clipped))
        way = gather_z(grid, low, len(orders))
        yield
        (came_in,), values = stage(grid, [next(way)], (yield))
        yield values
        ways = [gather_xy(grid, value, order) for value, order in zip(way.send(came_in), orders)]
        wanted = [next(way) for way in ways]
        for _ in range(2):
            came_in, values = stage(grid, wanted, (yield))
            came_in = lax.optimization_barrier(came_in)
            yield values
            wanted = [way.send(got) for way, got in zip(ways, came_in)]
        own = wanted
        early = [[grid.send(part[0], c=1)] for part in own]
        after = yield clipped, own
        last, _ = stage(grid, [[(piece, {"c": 1}) for piece in part[1:]] for part in own], after)
        other = [a + b for a, b in zip(early, last)]
        yield other

    ways = [section(0), section(1)]

    def run(stages):
        for _ in range(stages):
            for way in ways:
                next(way)
                way.send(())

    run(3)
    squares = [next(way) for way in ways]
    factors = clip_factor(sum_everywhere(jnp.stack(squares)))
    factors = lax.optimization_barrier(jnp.broadcast_to(factors[:, None, None], (2, 1, half)))
    for s in (0, 1):
        ways[s].send(factors[s])
    run(3)
    clipped, own = zip(*[next(way) for way in ways])
    (gate,) = project(grid, next_tokens, [{0: own[0]}], orders)
    other = [ways[0].send([]), ways[1].send([])]
    halves = [{1: other[0]}, {0: own[1], 1: other[1]}]
    state = (*clipped, first_moment, second_moment)
    next_hidden, new_first, new_second = project(grid, next_tokens, halves, orders, gate, state)
    return new_first, new_second, next_hidden


def solution(mesh):
    spec = P(AXES, None)
    return jax.shard_map(shards, mesh=mesh, in_specs=(spec,) * 6, out_specs=(spec,) * 3, check_vma=False)
```

```python
import functools
import math

import jax
import jax.numpy as jnp
from jax import lax
from jax.experimental import pallas as pl
from jax.experimental.pallas import tpu as pltpu
from jax.sharding import PartitionSpec as P

D = 2048
FF = 512
AXES = ("aa", "ba")
BF16 = jnp.bfloat16
F32 = jnp.float32
LANES = 128
LARGE = 60 * 1024 * 1024
SMALL = 14 * 1024 * 1024


class Grid:
    def __init__(self):
        outer, inner = lax.axis_size("aa"), lax.axis_size("ba")
        y = 1
        while y * y * 4 <= inner:
            y *= 2
        self.size = {"x": outer // 2, "c": 2, "z": inner // y, "y": y}

    def here(self, axis, step=0):
        a, b = lax.axis_index("aa"), lax.axis_index("ba")
        inner = self.size["c"] if axis in "xc" else self.size["y"]
        index = a if axis in "xc" else b
        return self.partner(axis, lax.div(index, inner) if axis in "xz" else lax.rem(index, inner), step)

    def partner(self, axis, at, step):
        return at ^ step if step else at

    def send(self, value, **steps):
        pairs = []
        for x in range(self.size["x"]):
            for c in range(self.size["c"]):
                for z in range(self.size["z"]):
                    for y in range(self.size["y"]):
                        here = {"x": x, "c": c, "z": z, "y": y}
                        there = {k: int(self.partner(k, v, steps.get(k, 0))) for k, v in here.items()}
                        pairs.append((self.index(here), self.index(there)))
        return lax.ppermute(value, AXES, pairs)

    def index(self, at):
        return ((at["x"] * self.size["c"] + at["c"]) * self.size["z"] + at["z"]) * self.size["y"] + at["y"]


def pick(value, axis, index):
    return lax.dynamic_index_in_dim(value, index, axis, keepdims=False)


def kernel_params(flops, moved, limit=LARGE):
    return dict(
        compiler_params=pltpu.CompilerParams(vmem_limit_bytes=limit),
        cost_estimate=pl.CostEstimate(flops=flops, bytes_accessed=moved, transcendentals=0),
    )


def column_block(grid, x, step, rows):
    return pl.ds(pl.multiple_of((x * 2 + grid.here("c", step)) * rows, rows), rows)


def product(block, cot):
    return lax.dot_general(block, cot, (((0,), (0,)), ((), ())), preferred_element_type=F32)


def cut_columns(total, cuts):
    bounds = [total * cut // 8 for cut in (0, *cuts, 8)]
    orders = ("xy", "yx") * (len(bounds) // 2)
    return [(order, slice(a, b)) for order, a, b in zip(orders, bounds, bounds[1:])]


def width_of(part):
    return part[1].stop - part[1].start


def sent_kernel(grid, parts, tokens_ref, cot_ref, *refs):
    outs, (tokens, cot, sems) = refs[:-3], refs[-3:]
    n, _, rows = tokens.shape
    half = cot.shape[1] // 2
    halves = [slice(0, half), slice(half, 2 * half)]
    cot_copies = [pltpu.make_async_copy(cot_ref.at[:, h], cot.at[:, h], sems.at[n + i]) for i, h in enumerate(halves)]
    copies = []
    for x in range(n):
        block = tokens_ref.at[:, column_block(grid, x, 1, rows)]
        copies.append(pltpu.make_async_copy(block, tokens.at[x], sems.at[x]))
    for copy in (cot_copies[0], copies[0], cot_copies[1], *copies[1:]):
        copy.start()
    for x in range(n):
        copies[x].wait()
        for h, copy in zip(halves, cot_copies):
            if x == 0:
                copy.wait()
            value = product(tokens[x], cot[:, h])
            for ref, (_, columns) in zip(outs, parts):
                if h.start <= columns.start < h.stop:
                    inner = slice(columns.start - h.start, columns.stop - h.start)
                    ref[pl.ds(x * rows, rows), :] = value[:, inner].astype(ref.dtype)


def sent_rows(grid, tokens, cot, parts):
    count, depth = tokens.shape
    n = grid.size["x"]
    rows = depth // (n * 2)
    return pl.pallas_call(
        functools.partial(sent_kernel, grid, parts),
        out_shape=[jax.ShapeDtypeStruct((n * rows, width_of(part)), BF16) for part in parts],
        in_specs=[pl.BlockSpec(memory_space=pltpu.HBM)] * 2,
        out_specs=[pl.BlockSpec(memory_space=pltpu.VMEM)] * len(parts),
        scratch_shapes=[
            pltpu.VMEM((n, count, rows), BF16),
            pltpu.VMEM(cot.shape, BF16),
            pltpu.SemaphoreType.DMA((n + 2,)),
        ],
        **kernel_params(2 * count * n * rows * cot.shape[1], count * n * rows * 2 + cot.size * 2, SMALL),
    )(*(pltpu.with_memory_space_constraint(v, pltpu.HBM) for v in (tokens, cot)))


def kept_product_kernel(grid, tokens, cot, out):
    rows = out.shape[0] // grid.size["x"]
    for x in range(grid.size["x"]):
        out[x * rows : (x + 1) * rows, :] = product(tokens[:, column_block(grid, x, 0, rows)], cot[...])


def kept_product(grid, tokens, cot):
    count, depth = tokens.shape
    whole = pl.BlockSpec(memory_space=pltpu.VMEM)
    return pl.pallas_call(
        functools.partial(kept_product_kernel, grid),
        out_shape=jax.ShapeDtypeStruct((depth // 2, cot.shape[1]), F32),
        in_specs=[whole] * 2,
        out_specs=whole,
        **kernel_params(count * depth * cot.shape[1], count * depth + cot.size * 2, SMALL),
    )(tokens, cot)


def kept_kernel(grid, parts, block_rows, value_ref, *refs):
    refs = list(refs)
    came = [refs.pop(0) for _ in parts]
    outs = [[refs.pop(0) for _ in range(1, grid.size[order[0]])] for order, _ in parts]
    outs = [[refs.pop(0), *others] for others in outs]
    *arrived, buffer, sems = refs
    nx, ny, nz = (grid.size[axis] for axis in "xyz")
    rows = buffer.shape[0]
    copies = [pltpu.make_async_copy(ref, arrived[k], sems.at[k]) for k, ref in enumerate(came)]
    for copy in copies:
        copy.start()
    for kx in range(nx):
        x = grid.here("x", kx)
        here = pl.ds(pl.multiple_of(x * rows, rows), rows)
        for k, (order, columns) in enumerate(parts):
            if kx == 0:
                copies[k].wait()
            wide = slice(0, columns.stop - columns.start)
            buffer[:, wide] = value_ref[here, columns] + arrived[k][here, :].astype(F32)
            for y in range(ny):
                out, at = (outs[k][kx], y) if order == "xy" else (outs[k][y], x)
                near = y if order == "xy" else grid.here("y", y)
                for z in range(nz):
                    start = pl.multiple_of((z * ny + near) * block_rows, block_rows)
                    out[at, z] = buffer[pl.ds(start, block_rows), wide].astype(out.dtype)


def kept_rows(grid, value, came, parts):
    nx, ny, nz = (grid.size[axis] for axis in "xyz")
    rows = value.shape[0] // nx
    block_rows = rows // (nz * ny)
    lead = {"xy": (ny, nz, block_rows), "yx": (nx, nz, block_rows)}
    shapes = [(*lead[part[0]], width_of(part)) for part in parts]
    counts = [grid.size[part[0][0]] - 1 for part in parts]
    out_shape = [jax.ShapeDtypeStruct(shape, BF16) for shape, n in zip(shapes, counts) for _ in range(n)]
    out_shape += [jax.ShapeDtypeStruct(shape, F32) for shape in shapes]
    whole = pl.BlockSpec(memory_space=pltpu.VMEM)
    outs = pl.pallas_call(
        functools.partial(kept_kernel, grid, parts, block_rows),
        out_shape=out_shape,
        in_specs=[whole] + [pl.BlockSpec(memory_space=pl.ANY)] * len(came),
        out_specs=[whole] * len(out_shape),
        scratch_shapes=[pltpu.VMEM(value.shape, BF16) for value in came]
        + [
            pltpu.VMEM((rows, max(width_of(part) for part in parts)), F32),
            pltpu.SemaphoreType.DMA((len(parts),)),
        ],
        **kernel_params(0, value.size * 12, SMALL),
    )(value, *came)
    outs = iter(outs)
    others = [[next(outs) for _ in range(n)] for n in counts]
    return [[next(outs), *values] for values in others]


def scatter_xy(grid, sums, order):
    one_axis, two_axis = order
    n_one, n_two = grid.size[one_axis], grid.size[two_axis]
    arriving = yield [(sums[one], {one_axis: one}) for one in range(1, n_one)]
    own = sums[0]
    for value in arriving:
        own = own + value.astype(F32)
    arriving = yield [
        (pick(own, 0, grid.here(two_axis, two)).astype(BF16), {two_axis: two}) for two in range(1, n_two)
    ]
    total = pick(own, 0, grid.here(two_axis))
    for value in arriving:
        total = total + value.astype(F32)
    yield total


def scatter_z(grid, totals):
    whole = jnp.concatenate(totals, axis=2)
    arriving = yield [
        (pick(whole, 0, grid.here("z", k)).astype(BF16), {"z": k}) for k in reversed(range(1, grid.size["z"]))
    ]
    total = pick(whole, 0, grid.here("z"))
    for value in arriving:
        total = total + value.astype(F32)
    yield total


def sum_everywhere(value):
    count = lax.axis_size("aa") * lax.axis_size("ba")
    terms = lax.all_to_all(jnp.broadcast_to(value, (count, *value.shape)), AXES, 0, 0, tiled=True)
    return jnp.sum(terms, axis=(0, 2))


def moments(clipped, first, second):
    return 0.9 * first + 0.1 * clipped, 0.95 * second + 0.05 * clipped * clipped


def clip_factor(square):
    return jnp.minimum(1.0, math.sqrt(D * FF) / jnp.sqrt(square + 1e-06))


def adam(clipped, weight, first, second):
    new_first, new_second = moments(clipped, first, second)
    corr_first = 1.0 - 0.9**10
    corr_second = 1.0 - 0.95**10
    updated = weight * (1.0 - 0.003 * 0.1) - 0.003 * (new_first / corr_first) / (
        jnp.sqrt(new_second / corr_second) + 1e-08
    )
    return updated.astype(BF16)


def gather_z(grid, low, widths):
    steps = range(1, grid.size["z"])
    pieces = yield [(low, {"z": k}) for k in reversed(steps)]
    pieces = [low] + pieces[::-1]
    starts = [sum(widths[:k]) for k in range(len(widths))]
    yield [jnp.stack([p[:, a : a + width] for p in pieces]) for a, width in zip(starts, widths)]


def gather_xy(grid, value, order):
    one_axis, two_axis = order
    pieces = yield [(value, {two_axis: two}) for two in range(1, grid.size[two_axis])]
    value = jnp.stack([value] + pieces)
    pieces = yield [(value, {one_axis: one}) for one in range(1, grid.size[one_axis])]
    yield [value] + pieces


def stage(grid, wanted):
    return [[grid.send(value, **steps) for value, steps in sends] for sends in wanted]


def overlaps(parts, half, which):
    found = []
    for p, (order, columns) in enumerate(parts):
        a, b = max(columns.start, which * half), min(columns.stop, (which + 1) * half)
        if a < b:
            inner = slice(a - columns.start, b - columns.start)
            found.append((p, order, inner, slice(a - which * half, b - which * half)))
    return found


def project_kernel(grid, plan, rows, finish, *refs):
    refs = list(refs)
    nx, ny, nz = (grid.size[axis] for axis in "xyz")
    tokens = refs.pop(0)
    pieces = [[[refs.pop(0) for _ in range(grid.size[order[0]])] for _, order, _, _ in cut] for _, _, cut in plan]
    if finish:
        earlier, *state = [refs.pop(0) for _ in range(5)]
        out, *new, held = refs
    else:
        out, held = refs
    block = nz * ny * rows

    @pl.when(pl.program_id(0) == 0)
    def _():
        if finish:
            *clipped, first, second = state
            start = 0
            for ref in clipped:
                at = slice(start, start + ref.shape[1])
                new[0][:, at], new[1][:, at] = moments(ref[...], first[:, at], second[:, at])
                start = at.stop
        for i, (_, _, cut) in enumerate(plan):
            for kx in range(nx):
                for ky in range(ny):
                    for kz in range(nz):
                        at = (grid.here("x", kx) * nz + grid.here("z", kz)) * ny + grid.here("y", ky)
                        at = pl.ds(pl.multiple_of(at * rows, rows), rows)
                        for piece, (_, order, inner, columns) in zip(pieces[i], cut):
                            one, two = (kx, ky) if order == "xy" else (ky, kx)
                            held[i, at, columns] = piece[one][two, kz, :, inner].astype(held.dtype)

    tile = pl.ds(pl.multiple_of(pl.program_id(0) * out.shape[0], out.shape[0]), out.shape[0])
    totals = [earlier[tile, :], None] if finish else [None]
    for i, (h, kc, _) in enumerate(plan):
        for x in range(nx):
            weight = held[i, x * block : (x + 1) * block, :].astype(BF16)
            term = jnp.dot(tokens[tile, column_block(grid, x, kc, block)], weight, preferred_element_type=F32)
            totals[h] = term if totals[h] is None else totals[h] + term
    value = totals[0]
    if finish:
        value = value / (1.0 + jnp.exp(-value)) * totals[1]
    out[...] = value.astype(out.dtype)


def project(grid, tokens, places, parts, half, earlier=None, state=()):
    count, depth = tokens.shape
    nx = grid.size["x"]
    block = depth // (nx * 2)
    plan = [(which, kc, overlaps(parts, half, which)) for which, kc, _ in places]
    flat = [piece for (_, _, cut), (_, _, table) in zip(plan, places) for p, *_ in cut for piece in table[p]]
    rows = flat[0].shape[2]
    tile = min(count, 512)
    held = BF16 if rows % 16 == 0 else F32
    finish = earlier is not None
    tiled = pl.BlockSpec((tile, half), lambda t: (t, 0))
    return pl.pallas_call(
        functools.partial(project_kernel, grid, plan, rows, finish),
        out_shape=[jax.ShapeDtypeStruct((count, half), BF16 if finish else F32)]
        + [jax.ShapeDtypeStruct(value.shape, F32) for value in state[-2:]],
        grid=(count // tile,),
        in_specs=[pl.BlockSpec(memory_space=pltpu.VMEM)] * (1 + len(flat) + finish + len(state)),
        out_specs=[tiled] + [pl.BlockSpec(value.shape, lambda t: (0, 0)) for value in state[-2:]],
        scratch_shapes=[pltpu.VMEM((len(plan), nx * block, half), held)],
        **kernel_params(
            2 * count * nx * block * len(plan) * half, count * depth * 2 + count * half * 8, SMALL
        ),
    )(tokens, *flat, *([earlier] if finish else []), *state)


def shards(tokens, grad_out, master_weight, first_moment, second_moment, next_tokens):
    grid = Grid()
    total = grad_out.shape[1]
    half = total // 2
    inward, outward = cut_columns(total, (2, 4, 6)), cut_columns(total, (2, 4, 6))

    came = [grid.send(value, c=1) for value in sent_rows(grid, tokens, grad_out, inward)]
    sums = kept_rows(grid, kept_product(grid, tokens, grad_out), came, inward)

    def scatter(first):
        ways = [scatter_xy(grid, sums[k], inward[k][0]) for k in (first, first + 1)]
        wanted = [next(way) for way in ways]
        for _ in range(2):
            came_in = lax.optimization_barrier(stage(grid, wanted))
            yield
            wanted = [way.send(got) for way, got in zip(ways, came_in)]
        way = scatter_z(grid, wanted)
        (came_in,) = stage(grid, [next(way)])
        yield
        yield way.send(came_in)

    def gather(first, grad, factor):
        parts = outward[first : first + 2]
        columns = slice(parts[0][1].start, parts[1][1].stop)
        clipped = grad[:, columns] * factor[:, columns]
        low = adam(clipped, *[value[:, columns] for value in (master_weight, first_moment, second_moment)])
        low, clipped = lax.optimization_barrier((low, clipped))
        way = gather_z(grid, low, [width_of(part) for part in parts])
        (came_in,) = stage(grid, [next(way)])
        yield
        ways = [gather_xy(grid, value, part[0]) for value, part in zip(way.send(came_in), parts)]
        wanted = [next(way) for way in ways]
        for _ in range(2):
            came_in = lax.optimization_barrier(stage(grid, wanted))
            yield
            wanted = [way.send(got) for way, got in zip(ways, came_in)]
        yield clipped, wanted, [[grid.send(piece, c=1) for piece in table] for table in wanted]

    def run(ways):
        for _ in range(3):
            for way in ways:
                next(way)
        return [next(way) for way in ways]

    grad = jnp.concatenate(run([scatter(0), scatter(2)]), axis=1)
    squares = jnp.sum((grad * grad).reshape(grad.shape[0], 2, -1, LANES), axis=(0, 2))
    factors = clip_factor(sum_everywhere(squares))
    factors = lax.optimization_barrier(jnp.broadcast_to(factors[:, None], (2, half)).reshape(1, total))
    (clipped_a, own_a, other_a), (clipped_b, own_b, other_b) = run([gather(0, grad, factors), gather(2, grad, factors)])
    own, other = own_a + own_b, other_a + other_b
    (gate,) = project(grid, next_tokens, [(0, 0, own)], outward, half)
    places = [(0, 1, other), (1, 0, own), (1, 1, other)]
    state = (clipped_a, clipped_b, first_moment, second_moment)
    next_hidden, new_first, new_second = project(grid, next_tokens, places, outward, half, gate, state)
    return new_first, new_second, next_hidden


def solution(mesh):
    spec = P(AXES, None)
    return jax.shard_map(shards, mesh=mesh, in_specs=(spec,) * 6, out_specs=(spec,) * 3, check_vma=False)
```

```python
import functools
import math

import jax
import jax.numpy as jnp
from jax import lax
from jax.experimental import pallas as pl
from jax.experimental.pallas import tpu as pltpu
from jax.sharding import PartitionSpec as P

D = 2048
FF = 512
AXES = ("aa", "ba")
BF16 = jnp.bfloat16
F32 = jnp.float32
LANES = 128
LARGE = 60 * 1024 * 1024
SMALL = 14 * 1024 * 1024


class Grid:
    def __init__(self):
        outer, inner = lax.axis_size("aa"), lax.axis_size("ba")
        y = 1
        while y * y * 4 <= inner:
            y *= 2
        self.size = {"x": outer // 2, "c": 2, "z": inner // y, "y": y}

    def here(self, axis, step=0):
        a, b = lax.axis_index("aa"), lax.axis_index("ba")
        inner = self.size["c"] if axis in "xc" else self.size["y"]
        index = a if axis in "xc" else b
        return self.partner(axis, lax.div(index, inner) if axis in "xz" else lax.rem(index, inner), step)

    def partner(self, axis, at, step):
        return at ^ step if step else at

    def send(self, value, **steps):
        pairs = []
        for x in range(self.size["x"]):
            for c in range(self.size["c"]):
                for z in range(self.size["z"]):
                    for y in range(self.size["y"]):
                        here = {"x": x, "c": c, "z": z, "y": y}
                        there = {k: int(self.partner(k, v, steps.get(k, 0))) for k, v in here.items()}
                        pairs.append((self.index(here), self.index(there)))
        return lax.ppermute(value, AXES, pairs)

    def index(self, at):
        return ((at["x"] * self.size["c"] + at["c"]) * self.size["z"] + at["z"]) * self.size["y"] + at["y"]


def pick(value, axis, index):
    return lax.dynamic_index_in_dim(value, index, axis, keepdims=False)


def kernel_params(flops, moved, limit=LARGE):
    return dict(
        compiler_params=pltpu.CompilerParams(vmem_limit_bytes=limit),
        cost_estimate=pl.CostEstimate(flops=flops, bytes_accessed=moved, transcendentals=0),
    )


def column_block(grid, x, step, rows):
    return pl.ds(pl.multiple_of((x * 2 + grid.here("c", step)) * rows, rows), rows)


def product(block, cot):
    return lax.dot_general(block, cot, (((0,), (0,)), ((), ())), preferred_element_type=F32)


def cut_columns(total, cuts):
    bounds = [total * cut // 8 for cut in (0, *cuts, 8)]
    orders = ("xy", "yx") * (len(bounds) // 2)
    return [(order, slice(a, b)) for order, a, b in zip(orders, bounds, bounds[1:])]


def width_of(part):
    return part[1].stop - part[1].start


def sent_kernel(grid, parts, tokens_ref, cot_ref, *refs):
    outs, (tokens, cot, sems) = refs[:-3], refs[-3:]
    n, _, rows = tokens.shape
    half = cot.shape[1] // 2
    halves = [slice(0, half), slice(half, 2 * half)]
    cot_copies = [pltpu.make_async_copy(cot_ref.at[:, h], cot.at[:, h], sems.at[n + i]) for i, h in enumerate(halves)]
    copies = []
    for x in range(n):
        block = tokens_ref.at[:, column_block(grid, x, 1, rows)]
        copies.append(pltpu.make_async_copy(block, tokens.at[x], sems.at[x]))
    for copy in (cot_copies[0], copies[0], cot_copies[1], *copies[1:]):
        copy.start()
    for x in range(n):
        copies[x].wait()
        for h, copy in zip(halves, cot_copies):
            if x == 0:
                copy.wait()
            value = product(tokens[x], cot[:, h])
            for ref, (_, columns) in zip(outs, parts):
                if h.start <= columns.start < h.stop:
                    inner = slice(columns.start - h.start, columns.stop - h.start)
                    ref[pl.ds(x * rows, rows), :] = value[:, inner].astype(ref.dtype)


def sent_rows(grid, tokens, cot, parts):
    count, depth = tokens.shape
    n = grid.size["x"]
    rows = depth // (n * 2)
    return pl.pallas_call(
        functools.partial(sent_kernel, grid, parts),
        out_shape=[jax.ShapeDtypeStruct((n * rows, width_of(part)), BF16) for part in parts],
        in_specs=[pl.BlockSpec(memory_space=pltpu.HBM)] * 2,
        out_specs=[pl.BlockSpec(memory_space=pltpu.VMEM)] * len(parts),
        scratch_shapes=[
            pltpu.VMEM((n, count, rows), BF16),
            pltpu.VMEM(cot.shape, BF16),
            pltpu.SemaphoreType.DMA((n + 2,)),
        ],
        **kernel_params(2 * count * n * rows * cot.shape[1], count * n * rows * 2 + cot.size * 2, SMALL),
    )(*(pltpu.with_memory_space_constraint(v, pltpu.HBM) for v in (tokens, cot)))


def kept_product_kernel(grid, tokens, cot, out):
    rows = out.shape[0] // grid.size["x"]
    for x in range(grid.size["x"]):
        out[x * rows : (x + 1) * rows, :] = product(tokens[:, column_block(grid, x, 0, rows)], cot[...])


def kept_product(grid, tokens, cot):
    count, depth = tokens.shape
    whole = pl.BlockSpec(memory_space=pltpu.VMEM)
    return pl.pallas_call(
        functools.partial(kept_product_kernel, grid),
        out_shape=jax.ShapeDtypeStruct((depth // 2, cot.shape[1]), F32),
        in_specs=[whole] * 2,
        out_specs=whole,
        **kernel_params(count * depth * cot.shape[1], count * depth + cot.size * 2, SMALL),
    )(tokens, cot)


def kept_kernel(grid, parts, block_rows, value_ref, *refs):
    refs = list(refs)
    came = [refs.pop(0) for _ in parts]
    outs = [[refs.pop(0) for _ in range(1, grid.size[order[0]])] for order, _ in parts]
    outs = [[refs.pop(0), *others] for others in outs]
    *arrived, buffer, sems = refs
    nx, ny, nz = (grid.size[axis] for axis in "xyz")
    rows = buffer.shape[0]
    copies = [pltpu.make_async_copy(ref, arrived[k], sems.at[k]) for k, ref in enumerate(came)]
    for copy in copies:
        copy.start()
    for kx in range(nx):
        x = grid.here("x", kx)
        here = pl.ds(pl.multiple_of(x * rows, rows), rows)
        for k, (order, columns) in enumerate(parts):
            if kx == 0:
                copies[k].wait()
            wide = slice(0, columns.stop - columns.start)
            buffer[:, wide] = value_ref[here, columns] + arrived[k][here, :].astype(F32)
            for y in range(ny):
                out, at = (outs[k][kx], y) if order == "xy" else (outs[k][y], x)
                near = y if order == "xy" else grid.here("y", y)
                for z in range(nz):
                    start = pl.multiple_of((z * ny + near) * block_rows, block_rows)
                    out[at, z] = buffer[pl.ds(start, block_rows), wide].astype(out.dtype)


def kept_rows(grid, value, came, parts):
    nx, ny, nz = (grid.size[axis] for axis in "xyz")
    rows = value.shape[0] // nx
    block_rows = rows // (nz * ny)
    lead = {"xy": (ny, nz, block_rows), "yx": (nx, nz, block_rows)}
    shapes = [(*lead[part[0]], width_of(part)) for part in parts]
    counts = [grid.size[part[0][0]] - 1 for part in parts]
    out_shape = [jax.ShapeDtypeStruct(shape, BF16) for shape, n in zip(shapes, counts) for _ in range(n)]
    out_shape += [jax.ShapeDtypeStruct(shape, F32) for shape in shapes]
    whole = pl.BlockSpec(memory_space=pltpu.VMEM)
    outs = pl.pallas_call(
        functools.partial(kept_kernel, grid, parts, block_rows),
        out_shape=out_shape,
        in_specs=[whole] + [pl.BlockSpec(memory_space=pl.ANY)] * len(came),
        out_specs=[whole] * len(out_shape),
        scratch_shapes=[pltpu.VMEM(value.shape, BF16) for value in came]
        + [
            pltpu.VMEM((rows, max(width_of(part) for part in parts)), F32),
            pltpu.SemaphoreType.DMA((len(parts),)),
        ],
        **kernel_params(0, value.size * 12, SMALL),
    )(value, *came)
    outs = iter(outs)
    others = [[next(outs) for _ in range(n)] for n in counts]
    return [[next(outs), *values] for values in others]


def scatter_xy(grid, sums, order):
    one_axis, two_axis = order
    n_one, n_two = grid.size[one_axis], grid.size[two_axis]
    arriving = yield [(sums[one], {one_axis: one}) for one in range(1, n_one)]
    own = sums[0]
    for value in arriving:
        own = own + value.astype(F32)
    arriving = yield [
        (pick(own, 0, grid.here(two_axis, two)).astype(BF16), {two_axis: two}) for two in range(1, n_two)
    ]
    total = pick(own, 0, grid.here(two_axis))
    for value in arriving:
        total = total + value.astype(F32)
    yield total


def scatter_z(grid, totals):
    whole = jnp.concatenate(totals, axis=2)
    arriving = yield [
        (pick(whole, 0, grid.here("z", k)).astype(BF16), {"z": k}) for k in list(range(1, grid.size["z"]))
    ]
    total = pick(whole, 0, grid.here("z"))
    for value in arriving:
        total = total + value.astype(F32)
    yield total


def sum_everywhere(value):
    count = lax.axis_size("aa") * lax.axis_size("ba")
    terms = lax.all_to_all(jnp.broadcast_to(value, (count, *value.shape)), AXES, 0, 0, tiled=True)
    return jnp.sum(terms, axis=(0, 2))


def moments(clipped, first, second):
    return 0.9 * first + 0.1 * clipped, 0.95 * second + 0.05 * clipped * clipped


def clip_factor(square):
    return jnp.minimum(1.0, math.sqrt(D * FF) / jnp.sqrt(square + 1e-06))


def adam(clipped, weight, first, second):
    new_first, new_second = moments(clipped, first, second)
    corr_first = 1.0 - 0.9**10
    corr_second = 1.0 - 0.95**10
    updated = weight * (1.0 - 0.003 * 0.1) - 0.003 * (new_first / corr_first) / (
        jnp.sqrt(new_second / corr_second) + 1e-08
    )
    return updated.astype(BF16)


def gather_z(grid, low, widths):
    steps = range(1, grid.size["z"])
    way = [grid.size["z"] - 1, *range(1, grid.size["z"] - 1)]
    pieces = yield [(low, {"z": k}) for k in way]
    pieces = [low] + [pieces[way.index(k)] for k in steps]
    starts = [sum(widths[:k]) for k in range(len(widths))]
    yield [jnp.stack([p[:, a : a + width] for p in pieces]) for a, width in zip(starts, widths)]


def gather_xy(grid, value, order):
    one_axis, two_axis = order
    pieces = yield [(value, {two_axis: two}) for two in range(1, grid.size[two_axis])]
    value = jnp.stack([value] + pieces)
    pieces = yield [(value, {one_axis: one}) for one in range(1, grid.size[one_axis])]
    yield [value] + pieces


def stage(grid, wanted):
    return [[grid.send(value, **steps) for value, steps in sends] for sends in wanted]


def overlaps(parts, half, which):
    found = []
    for p, (order, columns) in enumerate(parts):
        a, b = max(columns.start, which * half), min(columns.stop, (which + 1) * half)
        if a < b:
            inner = slice(a - columns.start, b - columns.start)
            found.append((p, order, inner, slice(a - which * half, b - which * half)))
    return found


def project_kernel(grid, plan, rows, before, finish, *refs):
    refs = list(refs)
    nx, ny, nz = (grid.size[axis] for axis in "xyz")
    tokens = refs.pop(0)
    pieces = [[[refs.pop(0) for _ in range(grid.size[order[0]])] for _, order, _, _ in cut] for _, _, cut in plan]
    earlier = refs.pop(0) if before else None
    state = [refs.pop(0) for _ in range(4)] if finish else []
    out, *new, held = refs
    block = nz * ny * rows

    @pl.when(pl.program_id(0) == 0)
    def _():
        if finish:
            *clipped, first, second = state
            start = 0
            for ref in clipped:
                at = slice(start, start + ref.shape[1])
                new[0][:, at], new[1][:, at] = moments(ref[...], first[:, at], second[:, at])
                start = at.stop
        for i, (_, _, cut) in enumerate(plan):
            for kx in range(nx):
                for ky in range(ny):
                    for kz in range(nz):
                        at = (grid.here("x", kx) * nz + grid.here("z", kz)) * ny + grid.here("y", ky)
                        at = pl.ds(pl.multiple_of(at * rows, rows), rows)
                        for piece, (_, order, inner, columns) in zip(pieces[i], cut):
                            one, two = (kx, ky) if order == "xy" else (ky, kx)
                            held[i, at, columns] = piece[one][two, kz, :, inner].astype(held.dtype)

    tile = pl.ds(pl.multiple_of(pl.program_id(0) * out.shape[0], out.shape[0]), out.shape[0])
    totals = [earlier[tile, :] if before else None, None]
    for i, (h, kc, _) in enumerate(plan):
        for x in range(nx):
            weight = held[i, x * block : (x + 1) * block, :].astype(BF16)
            term = jnp.dot(tokens[tile, column_block(grid, x, kc, block)], weight, preferred_element_type=F32)
            totals[h] = term if totals[h] is None else totals[h] + term
    value = totals[0]
    if finish:
        value = value / (1.0 + jnp.exp(-value)) * totals[1]
    out[...] = value.astype(out.dtype)


def project(grid, tokens, places, parts, half, earlier=None, state=()):
    count, depth = tokens.shape
    nx = grid.size["x"]
    block = depth // (nx * 2)
    plan = [(which, kc, overlaps(parts, half, which)) for which, kc, _ in places]
    flat = [piece for (_, _, cut), (_, _, table) in zip(plan, places) for p, *_ in cut for piece in table[p]]
    rows = flat[0].shape[2]
    tile = min(count, 512)
    held = BF16 if rows % 16 == 0 else F32
    before, finish = earlier is not None, bool(state)
    tiled = pl.BlockSpec((tile, half), lambda t: (t, 0))
    return pl.pallas_call(
        functools.partial(project_kernel, grid, plan, rows, before, finish),
        out_shape=[jax.ShapeDtypeStruct((count, half), BF16 if finish else F32)]
        + [jax.ShapeDtypeStruct(value.shape, F32) for value in state[-2:]],
        grid=(count // tile,),
        in_specs=[pl.BlockSpec(memory_space=pltpu.VMEM)] * (1 + len(flat) + before + len(state)),
        out_specs=[tiled] + [pl.BlockSpec(value.shape, lambda t: (0, 0)) for value in state[-2:]],
        scratch_shapes=[pltpu.VMEM((len(plan), nx * block, half), held)],
        **kernel_params(
            2 * count * nx * block * len(plan) * half, count * depth * 2 + count * half * 8, SMALL
        ),
    )(tokens, *flat, *([earlier] if before else []), *state)


def shards(tokens, grad_out, master_weight, first_moment, second_moment, next_tokens):
    grid = Grid()
    total = grad_out.shape[1]
    half = total // 2
    inward, outward = cut_columns(total, (2, 4, 6)), cut_columns(total, (2, 4, 6))

    came = [grid.send(value, c=1) for value in sent_rows(grid, tokens, grad_out, inward)]
    sums = kept_rows(grid, kept_product(grid, tokens, grad_out), came, inward)

    def scatter(first):
        ways = [scatter_xy(grid, sums[k], inward[k][0]) for k in (first, first + 1)]
        wanted = [next(way) for way in ways]
        for _ in range(2):
            came_in = lax.optimization_barrier(stage(grid, wanted))
            yield
            wanted = [way.send(got) for way, got in zip(ways, came_in)]
        way = scatter_z(grid, wanted)
        (came_in,) = stage(grid, [next(way)])
        yield
        yield way.send(came_in)

    def gather(first, grad, factor):
        parts = outward[first : first + 2]
        columns = slice(parts[0][1].start, parts[1][1].stop)
        clipped = grad[:, columns] * factor[:, columns]
        low = adam(clipped, *[value[:, columns] for value in (master_weight, first_moment, second_moment)])
        low, clipped = lax.optimization_barrier((low, clipped))
        way = gather_z(grid, low, [width_of(part) for part in parts])
        (came_in,) = stage(grid, [next(way)])
        yield
        ways = [gather_xy(grid, value, part[0]) for value, part in zip(way.send(came_in), parts)]
        wanted = [next(way) for way in ways]
        for _ in range(2):
            came_in = lax.optimization_barrier(stage(grid, wanted))
            yield
            wanted = [way.send(got) for way, got in zip(ways, came_in)]
        early = [[grid.send(table[0], c=1)] for table in wanted]
        after = yield clipped, wanted
        last = [table[1:] for table in wanted]
        if after is not None:
            last, _ = lax.optimization_barrier((last, after))
        yield [first + [grid.send(piece, c=1) for piece in rest] for first, rest in zip(early, last)]

    def run(ways):
        for _ in range(3):
            for way in ways:
                next(way)
        return [next(way) for way in ways]

    grad = jnp.concatenate(run([scatter(0), scatter(2)]), axis=1)
    squares = jnp.sum((grad * grad).reshape(grad.shape[0], 2, -1, LANES), axis=(0, 2))
    factors = clip_factor(sum_everywhere(squares))
    factors = lax.optimization_barrier(jnp.broadcast_to(factors[:, None], (2, half)).reshape(1, total))
    ways = [gather(0, grad, factors), gather(2, grad, factors)]
    (clipped_a, own_a), (clipped_b, own_b) = run(ways)
    own = own_a + own_b
    (gate,) = project(grid, next_tokens, [(0, 0, own)], outward, half)
    other = ways[0].send(gate) + ways[1].send(None)
    (gate,) = project(grid, next_tokens, [(0, 1, other)], outward, half, gate)
    state = (clipped_a, clipped_b, first_moment, second_moment)
    places = [(1, 0, own), (1, 1, other)]
    next_hidden, new_first, new_second = project(grid, next_tokens, places, outward, half, gate, state)
    return new_first, new_second, next_hidden


def solution(mesh):
    spec = P(AXES, None)
    return jax.shard_map(shards, mesh=mesh, in_specs=(spec,) * 6, out_specs=(spec,) * 3, check_vma=False)
```

```python
import functools
import math

import jax
import jax.numpy as jnp
from jax import lax
from jax.experimental import pallas as pl
from jax.experimental.pallas import tpu as pltpu
from jax.sharding import PartitionSpec as P

D = 2048
FF = 512
AXES = ("aa", "ba")
BF16 = jnp.bfloat16
F32 = jnp.float32
LANES = 128
LARGE = 60 * 1024 * 1024
SMALL = 14 * 1024 * 1024


class Grid:
    def __init__(self):
        outer, inner = lax.axis_size("aa"), lax.axis_size("ba")
        y = 1
        while y * y * 4 <= inner:
            y *= 2
        self.size = {"x": outer // 2, "c": 2, "z": inner // y, "y": y}

    def here(self, axis, step=0):
        a, b = lax.axis_index("aa"), lax.axis_index("ba")
        inner = self.size["c"] if axis in "xc" else self.size["y"]
        index = a if axis in "xc" else b
        return self.partner(axis, lax.div(index, inner) if axis in "xz" else lax.rem(index, inner), step)

    def partner(self, axis, at, step):
        return at ^ step if step else at

    def send(self, value, **steps):
        pairs = []
        for x in range(self.size["x"]):
            for c in range(self.size["c"]):
                for z in range(self.size["z"]):
                    for y in range(self.size["y"]):
                        here = {"x": x, "c": c, "z": z, "y": y}
                        there = {k: int(self.partner(k, v, steps.get(k, 0))) for k, v in here.items()}
                        pairs.append((self.index(here), self.index(there)))
        return lax.ppermute(value, AXES, pairs)

    def index(self, at):
        return ((at["x"] * self.size["c"] + at["c"]) * self.size["z"] + at["z"]) * self.size["y"] + at["y"]


def pick(value, axis, index):
    return lax.dynamic_index_in_dim(value, index, axis, keepdims=False)


def kernel_params(flops, moved, limit=LARGE):
    return dict(
        compiler_params=pltpu.CompilerParams(vmem_limit_bytes=limit),
        cost_estimate=pl.CostEstimate(flops=flops, bytes_accessed=moved, transcendentals=0),
    )


def column_block(grid, x, step, rows):
    return pl.ds(pl.multiple_of((x * 2 + grid.here("c", step)) * rows, rows), rows)


def product(block, cot):
    return lax.dot_general(block, cot, (((0,), (0,)), ((), ())), preferred_element_type=F32)


def cut_columns(total, cuts):
    bounds = [total * cut // 8 for cut in (0, *cuts, 8)]
    orders = ("xy", "yx") * (len(bounds) // 2)
    return [(order, slice(a, b)) for order, a, b in zip(orders, bounds, bounds[1:])]


def width_of(part):
    return part[1].stop - part[1].start


def sent_kernel(grid, parts, tokens_ref, cot_ref, *refs):
    outs, (tokens, cot, sems) = refs[:-3], refs[-3:]
    n, _, rows = tokens.shape
    half = cot.shape[1] // 2
    halves = [slice(0, half), slice(half, 2 * half)]
    cot_copies = [pltpu.make_async_copy(cot_ref.at[:, h], cot.at[:, h], sems.at[n + i]) for i, h in enumerate(halves)]
    copies = []
    for x in range(n):
        block = tokens_ref.at[:, column_block(grid, x, 1, rows)]
        copies.append(pltpu.make_async_copy(block, tokens.at[x], sems.at[x]))
    for copy in (cot_copies[0], copies[0], cot_copies[1], *copies[1:]):
        copy.start()
    for x in range(n):
        copies[x].wait()
        for h, copy in zip(halves, cot_copies):
            if x == 0:
                copy.wait()
            value = product(tokens[x], cot[:, h])
            for ref, (_, columns) in zip(outs, parts):
                if h.start <= columns.start < h.stop:
                    inner = slice(columns.start - h.start, columns.stop - h.start)
                    ref[pl.ds(x * rows, rows), :] = value[:, inner].astype(ref.dtype)


def sent_rows(grid, tokens, cot, parts):
    count, depth = tokens.shape
    n = grid.size["x"]
    rows = depth // (n * 2)
    return pl.pallas_call(
        functools.partial(sent_kernel, grid, parts),
        out_shape=[jax.ShapeDtypeStruct((n * rows, width_of(part)), BF16) for part in parts],
        in_specs=[pl.BlockSpec(memory_space=pltpu.HBM)] * 2,
        out_specs=[pl.BlockSpec(memory_space=pltpu.VMEM)] * len(parts),
        scratch_shapes=[
            pltpu.VMEM((n, count, rows), BF16),
            pltpu.VMEM(cot.shape, BF16),
            pltpu.SemaphoreType.DMA((n + 2,)),
        ],
        **kernel_params(2 * count * n * rows * cot.shape[1], count * n * rows * 2 + cot.size * 2, SMALL),
    )(*(pltpu.with_memory_space_constraint(v, pltpu.HBM) for v in (tokens, cot)))


def kept_product_kernel(grid, tokens, cot, out):
    rows = out.shape[0] // grid.size["x"]
    for x in range(grid.size["x"]):
        out[x * rows : (x + 1) * rows, :] = product(tokens[:, column_block(grid, x, 0, rows)], cot[...])


def kept_product(grid, tokens, cot):
    count, depth = tokens.shape
    whole = pl.BlockSpec(memory_space=pltpu.VMEM)
    return pl.pallas_call(
        functools.partial(kept_product_kernel, grid),
        out_shape=jax.ShapeDtypeStruct((depth // 2, cot.shape[1]), F32),
        in_specs=[whole] * 2,
        out_specs=whole,
        **kernel_params(count * depth * cot.shape[1], count * depth + cot.size * 2, SMALL),
    )(tokens, cot)


def kept_kernel(grid, parts, block_rows, value_ref, *refs):
    refs = list(refs)
    came = [refs.pop(0) for _ in parts]
    outs = [[refs.pop(0) for _ in range(1, grid.size[order[0]])] for order, _ in parts]
    outs = [[refs.pop(0), *others] for others in outs]
    *arrived, buffer, sems = refs
    nx, ny, nz = (grid.size[axis] for axis in "xyz")
    rows = buffer.shape[0]
    copies = [pltpu.make_async_copy(ref, arrived[k], sems.at[k]) for k, ref in enumerate(came)]
    for copy in copies:
        copy.start()
    for kx in range(nx):
        x = grid.here("x", kx)
        here = pl.ds(pl.multiple_of(x * rows, rows), rows)
        for k, (order, columns) in enumerate(parts):
            if kx == 0:
                copies[k].wait()
            wide = slice(0, columns.stop - columns.start)
            buffer[:, wide] = value_ref[here, columns] + arrived[k][here, :].astype(F32)
            for y in range(ny):
                out, at = (outs[k][kx], y) if order == "xy" else (outs[k][y], x)
                near = y if order == "xy" else grid.here("y", y)
                for z in range(nz):
                    start = pl.multiple_of((z * ny + near) * block_rows, block_rows)
                    out[at, z] = buffer[pl.ds(start, block_rows), wide].astype(out.dtype)


def kept_rows(grid, value, came, parts):
    nx, ny, nz = (grid.size[axis] for axis in "xyz")
    rows = value.shape[0] // nx
    block_rows = rows // (nz * ny)
    lead = {"xy": (ny, nz, block_rows), "yx": (nx, nz, block_rows)}
    shapes = [(*lead[part[0]], width_of(part)) for part in parts]
    counts = [grid.size[part[0][0]] - 1 for part in parts]
    out_shape = [jax.ShapeDtypeStruct(shape, BF16) for shape, n in zip(shapes, counts) for _ in range(n)]
    out_shape += [jax.ShapeDtypeStruct(shape, F32) for shape in shapes]
    whole = pl.BlockSpec(memory_space=pltpu.VMEM)
    outs = pl.pallas_call(
        functools.partial(kept_kernel, grid, parts, block_rows),
        out_shape=out_shape,
        in_specs=[whole] + [pl.BlockSpec(memory_space=pl.ANY)] * len(came),
        out_specs=[whole] * len(out_shape),
        scratch_shapes=[pltpu.VMEM(value.shape, BF16) for value in came]
        + [
            pltpu.VMEM((rows, max(width_of(part) for part in parts)), F32),
            pltpu.SemaphoreType.DMA((len(parts),)),
        ],
        **kernel_params(0, value.size * 12, SMALL),
    )(value, *came)
    outs = iter(outs)
    others = [[next(outs) for _ in range(n)] for n in counts]
    return [[next(outs), *values] for values in others]


def scatter_xy(grid, sums, order):
    one_axis, two_axis = order
    n_one, n_two = grid.size[one_axis], grid.size[two_axis]
    arriving = yield [(sums[one], {one_axis: one}) for one in range(1, n_one)]
    own = sums[0]
    for value in arriving:
        own = own + value.astype(F32)
    arriving = yield [
        (pick(own, 0, grid.here(two_axis, two)).astype(BF16), {two_axis: two}) for two in range(1, n_two)
    ]
    total = pick(own, 0, grid.here(two_axis))
    for value in arriving:
        total = total + value.astype(F32)
    yield total


def scatter_z(grid, totals):
    whole = jnp.concatenate(totals, axis=2)
    arriving = yield [
        (pick(whole, 0, grid.here("z", k)).astype(BF16), {"z": k}) for k in list(range(1, grid.size["z"]))
    ]
    total = pick(whole, 0, grid.here("z"))
    for value in arriving:
        total = total + value.astype(F32)
    yield total


def sum_everywhere(value):
    count = lax.axis_size("aa") * lax.axis_size("ba")
    terms = lax.all_to_all(jnp.broadcast_to(value, (count, *value.shape)), AXES, 0, 0, tiled=True)
    return jnp.sum(terms, axis=(0, 2))


def moments(clipped, first, second):
    return 0.9 * first + 0.1 * clipped, 0.95 * second + 0.05 * clipped * clipped


def clip_factor(square):
    return jnp.minimum(1.0, math.sqrt(D * FF) / jnp.sqrt(square + 1e-06))


def adam(clipped, weight, first, second):
    new_first, new_second = moments(clipped, first, second)
    corr_first = 1.0 - 0.9**10
    corr_second = 1.0 - 0.95**10
    updated = weight * (1.0 - 0.003 * 0.1) - 0.003 * (new_first / corr_first) / (
        jnp.sqrt(new_second / corr_second) + 1e-08
    )
    return updated.astype(BF16)


def gather_z(grid, low, widths):
    steps = range(1, grid.size["z"])
    way = [grid.size["z"] - 1, *range(1, grid.size["z"] - 1)]
    pieces = yield [(low, {"z": k}) for k in way]
    pieces = [low] + [pieces[way.index(k)] for k in steps]
    starts = [sum(widths[:k]) for k in range(len(widths))]
    yield [jnp.stack([p[:, a : a + width] for p in pieces]) for a, width in zip(starts, widths)]


def gather_xy(grid, value, order):
    one_axis, two_axis = order
    pieces = yield [(value, {two_axis: two}) for two in range(1, grid.size[two_axis])]
    value = jnp.stack([value] + pieces)
    pieces = yield [(value, {one_axis: one}) for one in range(1, grid.size[one_axis])]
    yield [value] + pieces


def stage(grid, wanted):
    return [[grid.send(value, **steps) for value, steps in sends] for sends in wanted]


def overlaps(parts, half, which):
    found = []
    for p, (order, columns) in enumerate(parts):
        a, b = max(columns.start, which * half), min(columns.stop, (which + 1) * half)
        if a < b:
            inner = slice(a - columns.start, b - columns.start)
            found.append((p, order, inner, slice(a - which * half, b - which * half)))
    return found


def project_kernel(grid, plan, rows, before, finish, *refs):
    refs = list(refs)
    nx, ny, nz = (grid.size[axis] for axis in "xyz")
    tokens = refs.pop(0)
    pieces = [[[refs.pop(0) for _ in range(grid.size[order[0]])] for _, order, _, _ in cut] for _, _, cut in plan]
    earlier = refs.pop(0) if before else None
    state = [refs.pop(0) for _ in range(4)] if finish else []
    out, *new, held = refs
    block = nz * ny * rows

    @pl.when(pl.program_id(0) == 0)
    def _():
        if finish:
            *clipped, first, second = state
            start = 0
            for ref in clipped:
                at = slice(start, start + ref.shape[1])
                new[0][:, at], new[1][:, at] = moments(ref[...], first[:, at], second[:, at])
                start = at.stop
        for i, (_, _, cut) in enumerate(plan):
            for kx in range(nx):
                for ky in range(ny):
                    for kz in range(nz):
                        at = (grid.here("x", kx) * nz + grid.here("z", kz)) * ny + grid.here("y", ky)
                        at = pl.ds(pl.multiple_of(at * rows, rows), rows)
                        for piece, (_, order, inner, columns) in zip(pieces[i], cut):
                            one, two = (kx, ky) if order == "xy" else (ky, kx)
                            held[i, at, columns] = piece[one][two, kz, :, inner].astype(held.dtype)

    tile = pl.ds(pl.multiple_of(pl.program_id(0) * out.shape[0], out.shape[0]), out.shape[0])
    totals = [earlier[tile, :] if before else None, None]
    for i, (h, kc, _) in enumerate(plan):
        for x in range(nx):
            weight = held[i, x * block : (x + 1) * block, :].astype(BF16)
            term = jnp.dot(tokens[tile, column_block(grid, x, kc, block)], weight, preferred_element_type=F32)
            totals[h] = term if totals[h] is None else totals[h] + term
    value = totals[0]
    if finish:
        value = value / (1.0 + jnp.exp(-value)) * totals[1]
    out[...] = value.astype(out.dtype)


def project(grid, tokens, places, parts, half, earlier=None, state=()):
    count, depth = tokens.shape
    nx = grid.size["x"]
    block = depth // (nx * 2)
    plan = [(which, kc, overlaps(parts, half, which)) for which, kc, _ in places]
    flat = [piece for (_, _, cut), (_, _, table) in zip(plan, places) for p, *_ in cut for piece in table[p]]
    rows = flat[0].shape[2]
    tile = min(count, 512)
    held = BF16 if rows % 16 == 0 else F32
    before, finish = earlier is not None, bool(state)
    tiled = pl.BlockSpec((tile, half), lambda t: (t, 0))
    return pl.pallas_call(
        functools.partial(project_kernel, grid, plan, rows, before, finish),
        out_shape=[jax.ShapeDtypeStruct((count, half), BF16 if finish else F32)]
        + [jax.ShapeDtypeStruct(value.shape, F32) for value in state[-2:]],
        grid=(count // tile,),
        in_specs=[pl.BlockSpec(memory_space=pltpu.VMEM)] * (1 + len(flat) + before + len(state)),
        out_specs=[tiled] + [pl.BlockSpec(value.shape, lambda t: (0, 0)) for value in state[-2:]],
        scratch_shapes=[pltpu.VMEM((len(plan), nx * block, half), held)],
        **kernel_params(
            2 * count * nx * block * len(plan) * half, count * depth * 2 + count * half * 8, SMALL
        ),
    )(tokens, *flat, *([earlier] if before else []), *state)


def shards(tokens, grad_out, master_weight, first_moment, second_moment, next_tokens):
    grid = Grid()
    total = grad_out.shape[1]
    half = total // 2
    inward, outward = cut_columns(total, (2, 4, 6)), cut_columns(total, (2, 4, 6))

    came = [grid.send(value, c=1) for value in sent_rows(grid, tokens, grad_out, inward)]
    sums = kept_rows(grid, kept_product(grid, tokens, grad_out), came, inward)

    def scatter(first):
        ways = [scatter_xy(grid, sums[k], inward[k][0]) for k in (first, first + 1)]
        wanted = [next(way) for way in ways]
        for _ in range(2):
            came_in = lax.optimization_barrier(stage(grid, wanted))
            yield
            wanted = [way.send(got) for way, got in zip(ways, came_in)]
        way = scatter_z(grid, wanted)
        (came_in,) = stage(grid, [next(way)])
        yield
        yield way.send(came_in)

    def gather(first, grad, factor):
        parts = outward[first : first + 2]
        columns = slice(parts[0][1].start, parts[1][1].stop)
        clipped = grad[:, columns] * factor[:, columns]
        low = adam(clipped, *[value[:, columns] for value in (master_weight, first_moment, second_moment)])
        low, clipped = lax.optimization_barrier((low, clipped))
        way = gather_z(grid, low, [width_of(part) for part in parts])
        (came_in,) = stage(grid, [next(way)])
        yield
        ways = [gather_xy(grid, value, part[0]) for value, part in zip(way.send(came_in), parts)]
        wanted = [next(way) for way in ways]
        for _ in range(2):
            came_in = lax.optimization_barrier(stage(grid, wanted))
            yield
            wanted = [way.send(got) for way, got in zip(ways, came_in)]
        early = [[grid.send(table[0], c=1)] for table in wanted]
        after = yield clipped, wanted
        last = [table[1:] for table in wanted]
        if after is not None:
            last[-1], _ = lax.optimization_barrier((last[-1], after))
        yield [first + [grid.send(piece, c=1) for piece in rest] for first, rest in zip(early, last)]

    def run(ways):
        for _ in range(3):
            for way in ways:
                next(way)
        return [next(way) for way in ways]

    grad = jnp.concatenate(run([scatter(0), scatter(2)]), axis=1)
    squares = jnp.sum((grad * grad).reshape(grad.shape[0], 2, -1, LANES), axis=(0, 2))
    factors = clip_factor(sum_everywhere(squares))
    factors = lax.optimization_barrier(jnp.broadcast_to(factors[:, None], (2, half)).reshape(1, total))
    ways = [gather(0, grad, factors), gather(2, grad, factors)]
    (clipped_a, own_a), (clipped_b, own_b) = run(ways)
    own = own_a + own_b
    (gate,) = project(grid, next_tokens, [(0, 0, own)], outward, half)
    other = ways[0].send(gate) + ways[1].send(None)
    (gate,) = project(grid, next_tokens, [(0, 1, other)], outward, half, gate)
    state = (clipped_a, clipped_b, first_moment, second_moment)
    places = [(1, 0, own), (1, 1, other)]
    next_hidden, new_first, new_second = project(grid, next_tokens, places, outward, half, gate, state)
    return new_first, new_second, next_hidden


def solution(mesh):
    spec = P(AXES, None)
    return jax.shard_map(shards, mesh=mesh, in_specs=(spec,) * 6, out_specs=(spec,) * 3, check_vma=False)
```

```python
import functools
import math

import jax
import jax.numpy as jnp
from jax import lax
from jax.experimental import pallas as pl
from jax.experimental.pallas import tpu as pltpu
from jax.sharding import PartitionSpec as P

D = 2048
FF = 512
AXES = ("aa", "ba")
BF16 = jnp.bfloat16
F32 = jnp.float32
LANES = 128
LARGE = 60 * 1024 * 1024
SMALL = 14 * 1024 * 1024


class Grid:
    def __init__(self):
        outer, inner = lax.axis_size("aa"), lax.axis_size("ba")
        y = 1
        while y * y * 4 <= inner:
            y *= 2
        self.size = {"x": outer // 2, "c": 2, "z": inner // y, "y": y}

    def here(self, axis, step=0):
        a, b = lax.axis_index("aa"), lax.axis_index("ba")
        inner = self.size["c"] if axis in "xc" else self.size["y"]
        index = a if axis in "xc" else b
        return self.partner(axis, lax.div(index, inner) if axis in "xz" else lax.rem(index, inner), step)

    def partner(self, axis, at, step):
        return at ^ step if step else at

    def send(self, value, **steps):
        pairs = []
        for x in range(self.size["x"]):
            for c in range(self.size["c"]):
                for z in range(self.size["z"]):
                    for y in range(self.size["y"]):
                        here = {"x": x, "c": c, "z": z, "y": y}
                        there = {k: int(self.partner(k, v, steps.get(k, 0))) for k, v in here.items()}
                        pairs.append((self.index(here), self.index(there)))
        return lax.ppermute(value, AXES, pairs)

    def index(self, at):
        return ((at["x"] * self.size["c"] + at["c"]) * self.size["z"] + at["z"]) * self.size["y"] + at["y"]


def pick(value, axis, index):
    return lax.dynamic_index_in_dim(value, index, axis, keepdims=False)


def kernel_params(flops, moved, limit=LARGE):
    return dict(
        compiler_params=pltpu.CompilerParams(vmem_limit_bytes=limit),
        cost_estimate=pl.CostEstimate(flops=flops, bytes_accessed=moved, transcendentals=0),
    )


def column_block(grid, x, step, rows):
    return pl.ds(pl.multiple_of((x * 2 + grid.here("c", step)) * rows, rows), rows)


def product(block, cot):
    return lax.dot_general(block, cot, (((0,), (0,)), ((), ())), preferred_element_type=F32)


def cut_columns(total, cuts):
    bounds = [total * cut // 8 for cut in (0, *cuts, 8)]
    orders = ("xy", "yx") * (len(bounds) // 2)
    return [(order, slice(a, b)) for order, a, b in zip(orders, bounds, bounds[1:])]


def width_of(part):
    return part[1].stop - part[1].start


def sent_kernel(grid, parts, tokens_ref, cot_ref, *refs):
    outs, (tokens, cot, sems) = refs[:-3], refs[-3:]
    n, _, rows = tokens.shape
    half = cot.shape[1] // 2
    halves = [slice(0, half), slice(half, 2 * half)]
    cot_copies = [pltpu.make_async_copy(cot_ref.at[:, h], cot.at[:, h], sems.at[n + i]) for i, h in enumerate(halves)]
    copies = []
    for x in range(n):
        block = tokens_ref.at[:, column_block(grid, x, 1, rows)]
        copies.append(pltpu.make_async_copy(block, tokens.at[x], sems.at[x]))
    for copy in (cot_copies[0], copies[0], cot_copies[1], *copies[1:]):
        copy.start()
    for x in range(n):
        copies[x].wait()
        for h, copy in zip(halves, cot_copies):
            if x == 0:
                copy.wait()
            value = product(tokens[x], cot[:, h])
            for ref, (_, columns) in zip(outs, parts):
                if h.start <= columns.start < h.stop:
                    inner = slice(columns.start - h.start, columns.stop - h.start)
                    ref[pl.ds(x * rows, rows), :] = value[:, inner].astype(ref.dtype)


def sent_rows(grid, tokens, cot, parts):
    count, depth = tokens.shape
    n = grid.size["x"]
    rows = depth // (n * 2)
    return pl.pallas_call(
        functools.partial(sent_kernel, grid, parts),
        out_shape=[jax.ShapeDtypeStruct((n * rows, width_of(part)), BF16) for part in parts],
        in_specs=[pl.BlockSpec(memory_space=pltpu.HBM)] * 2,
        out_specs=[pl.BlockSpec(memory_space=pltpu.VMEM)] * len(parts),
        scratch_shapes=[
            pltpu.VMEM((n, count, rows), BF16),
            pltpu.VMEM(cot.shape, BF16),
            pltpu.SemaphoreType.DMA((n + 2,)),
        ],
        **kernel_params(2 * count * n * rows * cot.shape[1], count * n * rows * 2 + cot.size * 2, SMALL),
    )(*(pltpu.with_memory_space_constraint(v, pltpu.HBM) for v in (tokens, cot)))


def kept_product_kernel(grid, tokens, cot, out):
    rows = out.shape[0] // grid.size["x"]
    for x in range(grid.size["x"]):
        out[x * rows : (x + 1) * rows, :] = product(tokens[:, column_block(grid, x, 0, rows)], cot[...])


def kept_product(grid, tokens, cot):
    count, depth = tokens.shape
    whole = pl.BlockSpec(memory_space=pltpu.VMEM)
    return pl.pallas_call(
        functools.partial(kept_product_kernel, grid),
        out_shape=jax.ShapeDtypeStruct((depth // 2, cot.shape[1]), F32),
        in_specs=[whole] * 2,
        out_specs=whole,
        **kernel_params(count * depth * cot.shape[1], count * depth + cot.size * 2, SMALL),
    )(tokens, cot)


def kept_kernel(grid, parts, block_rows, value_ref, *refs):
    refs = list(refs)
    came = [refs.pop(0) for _ in parts]
    outs = [[refs.pop(0) for _ in range(1, grid.size[order[0]])] for order, _ in parts]
    outs = [[refs.pop(0), *others] for others in outs]
    *arrived, buffer, sems = refs
    nx, ny, nz = (grid.size[axis] for axis in "xyz")
    rows = buffer.shape[0]
    copies = [pltpu.make_async_copy(ref, arrived[k], sems.at[k]) for k, ref in enumerate(came)]
    for copy in copies:
        copy.start()
    for kx in range(nx):
        x = grid.here("x", kx)
        here = pl.ds(pl.multiple_of(x * rows, rows), rows)
        for k, (order, columns) in enumerate(parts):
            if kx == 0:
                copies[k].wait()
            wide = slice(0, columns.stop - columns.start)
            buffer[:, wide] = value_ref[here, columns] + arrived[k][here, :].astype(F32)
            for y in range(ny):
                out, at = (outs[k][kx], y) if order == "xy" else (outs[k][y], x)
                near = y if order == "xy" else grid.here("y", y)
                for z in range(nz):
                    start = pl.multiple_of((z * ny + near) * block_rows, block_rows)
                    out[at, z] = buffer[pl.ds(start, block_rows), wide].astype(out.dtype)


def kept_rows(grid, value, came, parts):
    nx, ny, nz = (grid.size[axis] for axis in "xyz")
    rows = value.shape[0] // nx
    block_rows = rows // (nz * ny)
    lead = {"xy": (ny, nz, block_rows), "yx": (nx, nz, block_rows)}
    shapes = [(*lead[part[0]], width_of(part)) for part in parts]
    counts = [grid.size[part[0][0]] - 1 for part in parts]
    out_shape = [jax.ShapeDtypeStruct(shape, BF16) for shape, n in zip(shapes, counts) for _ in range(n)]
    out_shape += [jax.ShapeDtypeStruct(shape, F32) for shape in shapes]
    whole = pl.BlockSpec(memory_space=pltpu.VMEM)
    outs = pl.pallas_call(
        functools.partial(kept_kernel, grid, parts, block_rows),
        out_shape=out_shape,
        in_specs=[whole] + [pl.BlockSpec(memory_space=pl.ANY)] * len(came),
        out_specs=[whole] * len(out_shape),
        scratch_shapes=[pltpu.VMEM(value.shape, BF16) for value in came]
        + [
            pltpu.VMEM((rows, max(width_of(part) for part in parts)), F32),
            pltpu.SemaphoreType.DMA((len(parts),)),
        ],
        **kernel_params(0, value.size * 12, SMALL),
    )(value, *came)
    outs = iter(outs)
    others = [[next(outs) for _ in range(n)] for n in counts]
    return [[next(outs), *values] for values in others]


def scatter_xy(grid, sums, order):
    one_axis, two_axis = order
    n_one, n_two = grid.size[one_axis], grid.size[two_axis]
    arriving = yield [(sums[one], {one_axis: one}) for one in range(1, n_one)]
    own = sums[0]
    for value in arriving:
        own = own + value.astype(F32)
    arriving = yield [
        (pick(own, 0, grid.here(two_axis, two)).astype(BF16), {two_axis: two}) for two in range(1, n_two)
    ]
    total = pick(own, 0, grid.here(two_axis))
    for value in arriving:
        total = total + value.astype(F32)
    yield total


def scatter_z(grid, totals):
    whole = jnp.concatenate(totals, axis=2)
    arriving = yield [
        (pick(whole, 0, grid.here("z", k)).astype(BF16), {"z": k}) for k in list(range(1, grid.size["z"]))
    ]
    total = pick(whole, 0, grid.here("z"))
    for value in arriving:
        total = total + value.astype(F32)
    yield total


def sum_everywhere(value):
    count = lax.axis_size("aa") * lax.axis_size("ba")
    terms = lax.all_to_all(jnp.broadcast_to(value, (count, *value.shape)), AXES, 0, 0, tiled=True)
    return jnp.sum(terms, axis=(0, 2))


def moments(clipped, first, second):
    return 0.9 * first + 0.1 * clipped, 0.95 * second + 0.05 * clipped * clipped


def clip_factor(square):
    return jnp.minimum(1.0, math.sqrt(D * FF) / jnp.sqrt(square + 1e-06))


def adam(clipped, weight, first, second):
    new_first, new_second = moments(clipped, first, second)
    corr_first = 1.0 - 0.9**10
    corr_second = 1.0 - 0.95**10
    updated = weight * (1.0 - 0.003 * 0.1) - 0.003 * (new_first / corr_first) / (
        jnp.sqrt(new_second / corr_second) + 1e-08
    )
    return updated.astype(BF16)


def gather_z(grid, low, widths):
    steps = range(1, grid.size["z"])
    way = [grid.size["z"] - 1, *range(1, grid.size["z"] - 1)]
    pieces = yield [(low, {"z": k}) for k in way]
    pieces = [low] + [pieces[way.index(k)] for k in steps]
    starts = [sum(widths[:k]) for k in range(len(widths))]
    yield [jnp.stack([p[:, a : a + width] for p in pieces]) for a, width in zip(starts, widths)]


def gather_xy(grid, value, order):
    one_axis, two_axis = order
    pieces = yield [(value, {two_axis: two}) for two in range(1, grid.size[two_axis])]
    value = jnp.stack([value] + pieces)
    pieces = yield [(value, {one_axis: one}) for one in range(1, grid.size[one_axis])]
    yield [value] + pieces


def stage(grid, wanted):
    return [[grid.send(value, **steps) for value, steps in sends] for sends in wanted]


def overlaps(parts, half, which):
    found = []
    for p, (order, columns) in enumerate(parts):
        a, b = max(columns.start, which * half), min(columns.stop, (which + 1) * half)
        if a < b:
            inner = slice(a - columns.start, b - columns.start)
            found.append((p, order, inner, slice(a - which * half, b - which * half)))
    return found


def project_kernel(grid, plan, rows, before, finish, *refs):
    refs = list(refs)
    nx, ny, nz = (grid.size[axis] for axis in "xyz")
    tokens = refs.pop(0)
    pieces = [[[refs.pop(0) for _ in range(grid.size[order[0]])] for _, order, _, _ in cut] for _, _, cut in plan]
    earlier = refs.pop(0) if before else None
    state = [refs.pop(0) for _ in range(4)] if finish else []
    out, *new, held = refs
    block = nz * ny * rows

    @pl.when(pl.program_id(0) == 0)
    def _():
        if finish:
            *clipped, first, second = state
            start = 0
            for ref in clipped:
                at = slice(start, start + ref.shape[1])
                new[0][:, at], new[1][:, at] = moments(ref[...], first[:, at], second[:, at])
                start = at.stop
        for i, (_, _, cut) in enumerate(plan):
            for kx in range(nx):
                for ky in range(ny):
                    for kz in range(nz):
                        at = (grid.here("x", kx) * nz + grid.here("z", kz)) * ny + grid.here("y", ky)
                        at = pl.ds(pl.multiple_of(at * rows, rows), rows)
                        for piece, (_, order, inner, columns) in zip(pieces[i], cut):
                            one, two = (kx, ky) if order == "xy" else (ky, kx)
                            held[i, at, columns] = piece[one][two, kz, :, inner].astype(held.dtype)

    tile = pl.ds(pl.multiple_of(pl.program_id(0) * out.shape[0], out.shape[0]), out.shape[0])
    totals = [earlier[tile, :] if before else None, None]
    for i, (h, kc, _) in enumerate(plan):
        for x in range(nx):
            weight = held[i, x * block : (x + 1) * block, :].astype(BF16)
            term = jnp.dot(tokens[tile, column_block(grid, x, kc, block)], weight, preferred_element_type=F32)
            totals[h] = term if totals[h] is None else totals[h] + term
    value = totals[0]
    if finish:
        value = value / (1.0 + jnp.exp(-value)) * totals[1]
    out[...] = value.astype(out.dtype)


def project(grid, tokens, places, parts, half, earlier=None, state=()):
    count, depth = tokens.shape
    nx = grid.size["x"]
    block = depth // (nx * 2)
    plan = [(which, kc, overlaps(parts, half, which)) for which, kc, _ in places]
    flat = [piece for (_, _, cut), (_, _, table) in zip(plan, places) for p, *_ in cut for piece in table[p]]
    rows = flat[0].shape[2]
    tile = min(count, 512)
    held = BF16 if rows % 16 == 0 else F32
    before, finish = earlier is not None, bool(state)
    tiled = pl.BlockSpec((tile, half), lambda t: (t, 0))
    return pl.pallas_call(
        functools.partial(project_kernel, grid, plan, rows, before, finish),
        out_shape=[jax.ShapeDtypeStruct((count, half), BF16 if finish else F32)]
        + [jax.ShapeDtypeStruct(value.shape, F32) for value in state[-2:]],
        grid=(count // tile,),
        in_specs=[pl.BlockSpec(memory_space=pltpu.VMEM)] * (1 + len(flat) + before + len(state)),
        out_specs=[tiled] + [pl.BlockSpec(value.shape, lambda t: (0, 0)) for value in state[-2:]],
        scratch_shapes=[pltpu.VMEM((len(plan), nx * block, half), held)],
        **kernel_params(
            2 * count * nx * block * len(plan) * half, count * depth * 2 + count * half * 8, SMALL
        ),
    )(tokens, *flat, *([earlier] if before else []), *state)


def shards(tokens, grad_out, master_weight, first_moment, second_moment, next_tokens):
    grid = Grid()
    total = grad_out.shape[1]
    half = total // 2
    inward, outward = cut_columns(total, (2, 4, 6)), cut_columns(total, (2, 4, 6))

    came = [grid.send(value, c=1) for value in sent_rows(grid, tokens, grad_out, inward)]
    sums = kept_rows(grid, kept_product(grid, tokens, grad_out), came, inward)

    def scatter(first):
        ways = [scatter_xy(grid, sums[k], inward[k][0]) for k in (first, first + 1)]
        wanted = [next(way) for way in ways]
        for _ in range(2):
            came_in = lax.optimization_barrier(stage(grid, wanted))
            yield
            wanted = [way.send(got) for way, got in zip(ways, came_in)]
        way = scatter_z(grid, wanted)
        (came_in,) = stage(grid, [next(way)])
        yield
        yield way.send(came_in)

    def gather(first, grad, factor):
        parts = outward[first : first + 2]
        columns = slice(parts[0][1].start, parts[1][1].stop)
        clipped = grad[:, columns] * factor[:, columns]
        low = adam(clipped, *[value[:, columns] for value in (master_weight, first_moment, second_moment)])
        low, clipped = lax.optimization_barrier((low, clipped))
        way = gather_z(grid, low, [width_of(part) for part in parts])
        (came_in,) = stage(grid, [next(way)])
        yield
        ways = [gather_xy(grid, value, part[0]) for value, part in zip(way.send(came_in), parts)]
        wanted = [next(way) for way in ways]
        for _ in range(2):
            came_in = lax.optimization_barrier(stage(grid, wanted))
            yield
            wanted = [way.send(got) for way, got in zip(ways, came_in)]
        early = [[grid.send(table[0], c=1)] for table in wanted]
        after = yield clipped, wanted
        last = [table[1:] for table in wanted]
        if after is not None:
            last[0], _ = lax.optimization_barrier((last[0], after))
        yield [first + [grid.send(piece, c=1) for piece in rest] for first, rest in zip(early, last)]

    def run(ways):
        for _ in range(3):
            for way in ways:
                next(way)
        return [next(way) for way in ways]

    grad = jnp.concatenate(run([scatter(0), scatter(2)]), axis=1)
    squares = jnp.sum((grad * grad).reshape(grad.shape[0], 2, -1, LANES), axis=(0, 2))
    factors = clip_factor(sum_everywhere(squares))
    factors = lax.optimization_barrier(jnp.broadcast_to(factors[:, None], (2, half)).reshape(1, total))
    ways = [gather(0, grad, factors), gather(2, grad, factors)]
    (clipped_a, own_a), (clipped_b, own_b) = run(ways)
    own = own_a + own_b
    (gate,) = project(grid, next_tokens, [(0, 0, own)], outward, half)
    other = ways[0].send(gate) + ways[1].send(None)
    (gate,) = project(grid, next_tokens, [(0, 1, other)], outward, half, gate)
    state = (clipped_a, clipped_b, first_moment, second_moment)
    places = [(1, 0, own), (1, 1, other)]
    next_hidden, new_first, new_second = project(grid, next_tokens, places, outward, half, gate, state)
    return new_first, new_second, next_hidden


def solution(mesh):
    spec = P(AXES, None)
    return jax.shard_map(shards, mesh=mesh, in_specs=(spec,) * 6, out_specs=(spec,) * 3, check_vma=False)
```
